32 devices in a mesh: groups: 2 (over y), replica: 4 (over z), tensor: 4 (over x, core).
Axes of the slice: x: 2, y: 2, z: 4, core: 2. Of those that a mesh axis runs over, the one named last changes fastest.
Arguments:
- queries: bfloat16 [144, 8192], P(('groups', 'replica'), 'tensor'), parts along dimension 0, may hold values from -64 to 64
- past_cache: bfloat16 [2, 144, 128, 1024], P(None, ('groups', 'replica'), None, 'tensor'), parts along dimension 1, may hold values from -6 to 6
- lengths: int32 [144], P(('groups', 'replica')), parts along dimension 0, may hold values from 2 to 128, as said below
- live_counts: int32 [8], P(('groups', 'replica')), parts along dimension 0, may hold values from 1 to 16, as said below
- adapter_index: int32 [144], P(('groups', 'replica')), parts along dimension 0, may hold values from 0 to 15, as said below
- adapter_down: bfloat16 [16, 16, 8192], P('replica', None, 'tensor'), may hold values from -0.0625 to 0.0625
- adapter_up: bfloat16 [16, 16, 8192], P('replica', None, 'tensor'), may hold values from -6 to 6
Outputs:
- attention: bfloat16 [144, 8192], P(('groups', 'replica'), 'tensor'), parts along dimension 0
- adapted: bfloat16 [144, 8192], P(('groups', 'replica'), 'tensor'), parts along dimension 0
The draws below stay inside these ranges and needn't reach their ends.
There are 2 independent parts, one for each index of `groups`. The reference program is written for one: setup_inputs(seed, part) draws one part's arguments, and reference() takes and returns one part's arrays. A program takes and returns all parts, laid end to end along the dimension named above; an argument that names none is the same for every part. Nothing has to cross between parts.
Inputs may be any that keep to these rules, and one draw needn't show every extreme that they name: `adapter_index`: over the first 16 slots of all replicas, exactly 4 distinct adapters appear, homed on 4 distinct replicas. Each of the last 2 slots of a replica names an adapter outside that set; the homes (adapter a lives on replica a // 4) of one replica's last 2 slots are distinct, and some replica is the home of one such slot of every replica. `lengths`: some request has exactly 128. `live_counts`: some replica has exactly 16.
All inputs are finite; a program needn't handle non-finite values.
Results may differ from the reference program's by a relative error of at most 0.008.
Values may be sent and summed in bfloat16 or wider, within the bound.
No kernel may reach another device: no remote copies, remote signals or barrier semaphores. Data moves between devices by JAX's collectives and lax.ppermute only.
A program may use at most 64 MiB of HBM per device.

```python
import math
import jax
import jax.numpy as jnp
from jax import lax

D = 8192
HEADS = 64
KV_HEADS = 8
HEAD_DIM = 128
RANK = 16
ADP_DEV = 4
STAY = 16
CONTEXT = 128
HOT = 4
MIG = 2
B_DEV = 18
ADAPTERS = 16
REQUESTS = 72
N_REPLICA = 4


def routing(key):
    base = jax.random.fold_in(key, 11)
    streams = jax.random.split(base, 8)
    replicas = N_REPLICA
    lower_half = replicas // 2
    hot_homes = jax.random.permutation(streams[0], replicas)[:HOT].astype(jnp.int32)
    hot_local = jax.random.randint(streams[1], (HOT,), 0, ADP_DEV, dtype=jnp.int32)
    hot_ids = hot_homes * ADP_DEV + hot_local
    marks = jnp.full((replicas,), -1, jnp.int32).at[hot_homes].set(hot_local)
    picks = jax.random.randint(streams[2], (replicas, STAY), 0, HOT, dtype=jnp.int32)
    lower_picks = jax.random.randint(jax.random.fold_in(base, 101), (replicas, STAY), 1, HOT, dtype=jnp.int32)
    row_ids = jnp.arange(replicas, dtype=jnp.int32)
    picks = jnp.where((row_ids < lower_half)[:, None], lower_picks, picks)
    stay_ids = hot_ids[picks]
    first_row = jax.random.randint(streams[3], (), lower_half, replicas, dtype=jnp.int32)
    stay_ids = stay_ids.at[first_row, :HOT].set(hot_ids)
    full_home = jax.random.randint(streams[4], (), 0, replicas, dtype=jnp.int32)

    def choose(row_key):
        order = jax.random.permutation(row_key, replicas).astype(jnp.int32)[:MIG]
        present = jnp.any(order == full_home)
        return jnp.where(present, order, order.at[MIG - 1].set(full_home))
    targets = jax.vmap(choose)(jax.random.split(streams[5], replicas))
    spare = jax.random.randint(streams[6], (replicas, MIG), 0, ADP_DEV - 1, dtype=jnp.int32)
    loose = jax.random.randint(streams[7], (replicas, MIG), 0, ADP_DEV, dtype=jnp.int32)
    marked = marks[targets]
    local = jnp.where(marked < 0, loose, spare + (spare >= marked).astype(jnp.int32))
    moved_ids = targets * ADP_DEV + local
    return jnp.concatenate([stay_ids, moved_ids], axis=1).reshape(REQUESTS)


def draw_adapter_index(key, part):
    return routing(key)


def draw_lengths(key, part):
    base = jax.random.fold_in(key, 23)
    values = jax.random.randint(base, (REQUESTS,), 2, CONTEXT + 1, dtype=jnp.int32)
    position = jax.random.randint(jax.random.fold_in(base, 1), (), 0, REQUESTS, dtype=jnp.int32)
    return values.at[position].set(CONTEXT)


def draw_live_counts(key, part):
    base = jax.random.fold_in(key, 29)
    values = jax.random.randint(base, (N_REPLICA,), 1, STAY + 1, dtype=jnp.int32)
    position = jax.random.randint(jax.random.fold_in(base, 1), (), 0, N_REPLICA, dtype=jnp.int32)
    return values.at[position].set(STAY)


def paired_draws(key):
    base = jax.random.fold_in(key, 37)
    streams = jax.random.split(base, 2)
    width = KV_HEADS * HEAD_DIM
    queries = jax.random.truncated_normal(streams[0], -6.0, 6.0, (REQUESTS, HEADS * HEAD_DIM), jnp.float32)
    cache = jax.random.truncated_normal(streams[1], -6.0, 6.0, (2, REQUESTS, CONTEXT, width), jnp.float32)
    return (queries, cache)


def draw_queries(key, part):
    return paired_draws(key)[0].astype(jnp.bfloat16)


def draw_past_cache(key, part):
    return paired_draws(key)[1].astype(jnp.bfloat16)


def block_scale(rng, dims, cuts, low, top_value):
    gain, own = 1.0, jax.random.fold_in(rng, 6)
    for dim, parts in cuts:
        steps = jnp.exp(jax.random.uniform(jax.random.fold_in(own, dim), (parts,), jnp.float32, low / len(cuts), top_value / len(cuts)))
        gain = gain * jnp.repeat(steps, dims[dim] // parts).reshape([-1 if axis == dim else 1 for axis in range(len(dims))])
    return gain


def noise(key, extent, spread, limit, shards=(), kind=jnp.bfloat16):
    entries = spread * jax.random.normal(key, extent, jnp.float32)
    if shards:
        entries = entries * block_scale(key, extent, shards, -0.22, 0.18)
    return jnp.clip(entries, -limit, limit).astype(kind)


def setup_inputs(seed: int = 0, part: int = 0) -> dict:
    key_list = jax.random.split(jax.random.key(seed), 8)
    part_splits = jax.random.split(jax.random.fold_in(key_list[7], part), 8)
    queries = draw_queries(jax.random.fold_in(jax.random.fold_in(key_list[7], part), 71), part)
    past_cache = draw_past_cache(jax.random.fold_in(jax.random.fold_in(key_list[7], part), 71), part)
    lengths = draw_lengths(jax.random.fold_in(jax.random.fold_in(key_list[7], part), 71), part)
    live_counts = draw_live_counts(jax.random.fold_in(jax.random.fold_in(key_list[7], part), 71), part)
    adapter_index = draw_adapter_index(jax.random.fold_in(jax.random.fold_in(key_list[7], part), 71), part)
    adapter_down = noise(key_list[5], (ADAPTERS, RANK, HEADS * HEAD_DIM), (HEADS * HEAD_DIM) ** -0.5, 0.0625, ((0, 4), (2, 4)))
    adapter_up = noise(key_list[6], (ADAPTERS, RANK, D), 1.0, 6.0, ((0, 4), (2, 4)))
    return dict(queries=queries, past_cache=past_cache, lengths=lengths, live_counts=live_counts, adapter_index=adapter_index, adapter_down=adapter_down, adapter_up=adapter_up)


SCALING = 2.0

def attend_block(queries, keys, values, visible):
    count = queries.shape[0]
    key_width = keys.shape[-1]
    key_heads = key_width // HEAD_DIM
    group_size = queries.shape[1] // key_width
    context = keys.shape[1]
    query_rows = queries.astype(jnp.float32).reshape(count, key_heads, group_size, HEAD_DIM)
    key_rows = keys.astype(jnp.float32).reshape(count, context, key_heads, HEAD_DIM)
    value_rows = values.astype(jnp.float32).reshape(count, context, key_heads, HEAD_DIM)
    scores = jnp.einsum('nhgd,nlhd->nhgl', query_rows, key_rows) / math.sqrt(HEAD_DIM)
    scores = jnp.where(visible[:, None, None, :], scores, -jnp.inf)
    peak = lax.optimization_barrier(jnp.max(scores, axis=-1, keepdims=True))
    raised = jnp.exp(scores - peak)
    weights = (raised / lax.optimization_barrier(jnp.sum(raised, axis=-1, keepdims=True))).astype(jnp.bfloat16)
    mixed = jnp.einsum('nhgl,nlhd->nhgd', weights.astype(jnp.float32), value_rows)
    return mixed.reshape(count, key_heads * group_size * HEAD_DIM)

def reference(queries, past_cache, lengths, live_counts, adapter_index, adapter_down, adapter_up):
    requests = queries.shape[0]
    blocks = requests // B_DEV
    width = past_cache.shape[-1]
    slot_index = jnp.arange(requests, dtype=jnp.int32) % B_DEV
    owner = jnp.arange(requests, dtype=jnp.int32) // B_DEV
    alive = (slot_index >= STAY) | (slot_index < live_counts[owner])
    position = jnp.arange(CONTEXT, dtype=jnp.int32)
    zero = jnp.zeros((), jnp.int32)

    def one_block(block):
        start = (block * B_DEV).astype(jnp.int32)
        block_queries = lax.dynamic_slice_in_dim(queries, start, B_DEV, 0)
        block_cache = lax.dynamic_slice(past_cache, (zero, start, zero, zero), (2, B_DEV, CONTEXT, width))
        block_lengths = lax.dynamic_slice_in_dim(lengths, start, B_DEV, 0)
        block_alive = lax.dynamic_slice_in_dim(alive, start, B_DEV, 0)
        visible = position[None, :] < block_lengths[:, None]
        mixed = attend_block(block_queries, block_cache[0], block_cache[1], visible)
        attention = jnp.where(block_alive[:, None], mixed, 0.0).astype(jnp.bfloat16)
        chosen = lax.dynamic_slice_in_dim(adapter_index, start, B_DEV, 0)
        down_rows = adapter_down[chosen].astype(jnp.float32)
        up_rows = adapter_up[chosen].astype(jnp.float32)
        rank_rows = jnp.einsum('nc,nrc->nr', attention.astype(jnp.float32), down_rows)
        adapted = (SCALING * jnp.einsum('nr,nrc->nc', rank_rows, up_rows)).astype(jnp.bfloat16)
        return (attention, adapted)
    attention, adapted = lax.map(one_block, jnp.arange(blocks, dtype=jnp.int32))
    return (attention.reshape(requests, -1), adapted.reshape(requests, -1))
```

```python
import functools
import math

import jax
import jax.numpy as jnp
from jax import lax
from jax.experimental import pallas as pl
from jax.experimental.pallas import tpu as pltpu
from jax.sharding import PartitionSpec as P

HEAD_DIM = 128
STAY = 16
SCALING = 2.0
LANES = 128
DIGIT = 7

VMEM = pl.BlockSpec(memory_space=pltpu.VMEM)
SMEM = pl.BlockSpec(memory_space=pltpu.SMEM)
ANY = pl.BlockSpec(memory_space=pl.ANY)


def chunks_of(slots):
    for parts in (3, 4, 2):
        if slots % parts == 0:
            return parts
    return 1


def attend_kernel(q_ref, cache_ref, lengths_ref, live_ref, index_ref, rows_ref, keys, values, q_rows, o_rows, sems):
    slots, cols = q_ref.shape
    heads = cols // HEAD_DIM
    context, width = keys.shape[1:]
    key_heads = width // HEAD_DIM
    group = heads // key_heads
    parts = chunks_of(slots)
    step = slots // parts
    copies = []
    for side, buffer in enumerate((keys, values)):
        for part in range(parts):
            span = pl.ds(part * step, step)
            copy = pltpu.make_async_copy(cache_ref.at[side, span], buffer.at[span], sems.at[side, part])
            copy.start()
            copies.append(copy)
    for head in range(heads):
        block = q_ref[:, head * HEAD_DIM : (head + 1) * HEAD_DIM]
        q_rows[pl.ds(head, slots, stride=heads), :] = block.astype(jnp.float32)
    owner = lax.broadcasted_iota(jnp.int32, (heads, HEAD_DIM), 0) // group
    position = lax.broadcasted_iota(jnp.int32, (heads, context), 1)
    weights = []
    for slot in range(slots):
        if slot % step == 0:
            copies[slot // step].wait()
        rows = q_rows[slot * heads : (slot + 1) * heads, :]
        wide = [jnp.where(owner == k, rows, 0.0) for k in range(key_heads)]
        wide = jnp.concatenate(wide, axis=1).astype(jnp.bfloat16)
        scores = lax.dot_general(
            wide, keys[slot], (((1,), (1,)), ((), ())), preferred_element_type=jnp.float32
        ) / math.sqrt(HEAD_DIM)
        scores = jnp.where(position < lengths_ref[slot], scores, -jnp.inf)
        raised = jnp.exp(scores - jnp.max(scores, axis=-1, keepdims=True))
        weights.append((raised / jnp.sum(raised, axis=-1, keepdims=True)).astype(jnp.bfloat16))
    live = live_ref[0]
    for slot in range(slots):
        if slot % step == 0:
            copies[parts + slot // step].wait()
        mixed = jnp.dot(weights[slot], values[slot], preferred_element_type=jnp.float32)
        rows = mixed[:, :HEAD_DIM]
        for k in range(1, key_heads):
            rows = jnp.where(owner == k, mixed[:, k * HEAD_DIM : (k + 1) * HEAD_DIM], rows)
        if slot < STAY:
            rows = jnp.where(slot < live, rows, 0.0)
        o_rows[slot * heads : (slot + 1) * heads, :] = rows
    rows_ref[: slots * heads, :] = o_rows[...].astype(jnp.bfloat16)
    lane = lax.broadcasted_iota(jnp.int32, (16, LANES), 1)
    line = lax.broadcasted_iota(jnp.int32, (16, LANES), 0)
    index = jnp.zeros((16, LANES), jnp.int32)
    for slot in range(slots):
        index = jnp.where(lane == slot, index_ref[slot], index)
    digits = jnp.where(line == 0, index >> DIGIT, index & ((1 << DIGIT) - 1))
    rows_ref[slots * heads :, :] = digits.astype(jnp.float32).astype(jnp.bfloat16)


def attend(queries, past_cache, lengths, live_counts, adapter_index):
    slots, cols = queries.shape
    heads = cols // HEAD_DIM
    buffer = pltpu.VMEM(past_cache.shape[1:], past_cache.dtype)
    return pl.pallas_call(
        attend_kernel,
        out_shape=jax.ShapeDtypeStruct((slots * heads + 16, HEAD_DIM), jnp.bfloat16),
        in_specs=[VMEM, ANY, SMEM, SMEM, SMEM],
        out_specs=VMEM,
        scratch_shapes=[
            buffer,
            buffer,
            pltpu.VMEM((slots * heads, HEAD_DIM), jnp.float32),
            pltpu.VMEM((slots * heads, HEAD_DIM), jnp.float32),
            pltpu.SemaphoreType.DMA((2, chunks_of(slots))),
        ],
        cost_estimate=pl.CostEstimate(
            flops=4 * past_cache.size * heads, bytes_accessed=2 * past_cache.size, transcendentals=0
        ),
        name="attend",
    )(queries, past_cache, lengths, live_counts, adapter_index)


def unfold_kernel(slots, heads, rows_ref, out_ref, flat):
    flat[...] = rows_ref[: slots * heads, :].astype(jnp.float32)
    for head in range(heads):
        out_ref[:, head * HEAD_DIM : (head + 1) * HEAD_DIM] = flat[
            pl.ds(head, slots, stride=heads), :
        ].astype(out_ref.dtype)


def unfold(rows, slots, heads):
    return pl.pallas_call(
        functools.partial(unfold_kernel, slots, heads),
        out_shape=jax.ShapeDtypeStruct((slots, heads * HEAD_DIM), jnp.bfloat16),
        in_specs=[VMEM],
        out_specs=VMEM,
        scratch_shapes=[pltpu.VMEM((slots * heads, HEAD_DIM), jnp.float32)],
        name="unfold",
    )(rows)


def lower_kernel(slots, heads, pad, sources, base_ref, down_ref, *refs):
    rows_refs = refs[:sources]
    partial_ref, index_ref, flat, wide = refs[sources:]
    local_count, rank, cols = down_ref.shape
    for source in range(sources):
        flat[source, : slots * heads, :] = rows_refs[source][: slots * heads, :].astype(jnp.float32)
        if pad > slots:
            flat[source, slots * heads :, :] = jnp.zeros(((pad - slots) * heads, HEAD_DIM), jnp.float32)
        digits = rows_refs[source][slots * heads :, :].astype(jnp.float32).astype(jnp.int32)
        index = (digits[0:1, :] << DIGIT) + digits[1:2, :]
        index_ref[:, source * pad : (source + 1) * pad] = index[:, :pad]
    for source in range(sources):
        for head in range(heads):
            wide[source * pad : (source + 1) * pad, head * HEAD_DIM : (head + 1) * HEAD_DIM] = flat[
                source, pl.ds(head, pad, stride=heads), :
            ].astype(jnp.bfloat16)
    down = down_ref[...].reshape(local_count * rank, cols)
    every = lax.dot_general(down, wide[...], (((1,), (1,)), ((), ())), preferred_element_type=jnp.float32)
    total = jnp.zeros((rank, sources * pad), jnp.float32)
    for local in range(local_count):
        mine = index_ref[...] == base_ref[0] + local
        total += jnp.where(mine, every[local * rank : (local + 1) * rank, :], 0.0)
    partial_ref[...] = total


def lower(base, down, rows, slots, heads, pad):
    sources = len(rows)
    lanes = sources * pad
    cols = heads * HEAD_DIM
    return pl.pallas_call(
        functools.partial(lower_kernel, slots, heads, pad, sources),
        out_shape=(
            jax.ShapeDtypeStruct((down.shape[1], lanes), jnp.float32),
            jax.ShapeDtypeStruct((1, lanes), jnp.int32),
        ),
        in_specs=[SMEM] + [VMEM] * (1 + sources),
        out_specs=(VMEM, VMEM),
        scratch_shapes=[
            pltpu.VMEM((sources, pad * heads, HEAD_DIM), jnp.float32),
            pltpu.VMEM((lanes, cols), jnp.bfloat16),
        ],
        compiler_params=pltpu.CompilerParams(vmem_limit_bytes=32 * 2**20),
        name="lower",
    )(base, down, *rows)


def raise_kernel(slots, heads, pad, sources, base_ref, index_ref, up_ref, *refs):
    tensor = len(refs) - sources - 1
    partials = refs[:tensor]
    outs = refs[tensor : tensor + sources]
    flat = refs[-1]
    local_count, rank, cols = up_ref.shape
    total = partials[0][...]
    for other in partials[1:]:
        total += other[...]
    total = SCALING * total
    high = total.astype(jnp.bfloat16).astype(jnp.float32)
    spread = []
    for part in (high, total - high):
        for local in range(local_count):
            mine = index_ref[...] == base_ref[0] + local
            spread.append(jnp.where(mine, part, 0.0))
    spread = jnp.concatenate(spread, axis=0).astype(jnp.bfloat16)
    up = up_ref[...].reshape(local_count * rank, cols)
    up = jnp.concatenate([up, up], axis=0)
    block = min(sources, max(1, LANES // pad))
    for first in range(0, sources, block):
        count = min(block, sources - first)
        part = spread[:, first * pad : (first + count) * pad]
        wide = lax.dot_general(part, up, (((0,), (0,)), ((), ())), preferred_element_type=jnp.float32)
        for source in range(count):
            for head in range(heads):
                flat[source, pl.ds(head, slots, stride=heads), :] = wide[
                    source * pad : source * pad + slots, head * HEAD_DIM : (head + 1) * HEAD_DIM
                ]
        for source in range(count):
            outs[first + source][...] = flat[source].astype(jnp.bfloat16)


def raise_rows(base, index, up, partials, slots, heads, pad, sources):
    block = min(sources, max(1, LANES // pad))
    return pl.pallas_call(
        functools.partial(raise_kernel, slots, heads, pad, sources),
        out_shape=[jax.ShapeDtypeStruct((slots * heads, HEAD_DIM), jnp.bfloat16)] * sources,
        in_specs=[SMEM] + [VMEM] * (2 + len(partials)),
        out_specs=[VMEM] * sources,
        scratch_shapes=[pltpu.VMEM((block, slots * heads, HEAD_DIM), jnp.float32)],
        compiler_params=pltpu.CompilerParams(vmem_limit_bytes=32 * 2**20),
        name="raise_rows",
    )(base, index, up, *partials)


def merge_kernel(slots, heads, *refs):
    rows_refs, out_ref, flat = refs[:-2], refs[-2], refs[-1]
    total = rows_refs[0][...].astype(jnp.float32)
    for other in rows_refs[1:]:
        total += other[...].astype(jnp.float32)
    flat[...] = total
    for head in range(heads):
        out_ref[:, head * HEAD_DIM : (head + 1) * HEAD_DIM] = flat[
            pl.ds(head, slots, stride=heads), :
        ].astype(out_ref.dtype)


def merge(rows, slots, heads):
    return pl.pallas_call(
        functools.partial(merge_kernel, slots, heads),
        out_shape=jax.ShapeDtypeStruct((slots, heads * HEAD_DIM), jnp.bfloat16),
        in_specs=[VMEM] * len(rows),
        out_specs=VMEM,
        scratch_shapes=[pltpu.VMEM((slots * heads, HEAD_DIM), jnp.float32)],
        name="merge",
    )(*rows)


def shift(block, axis, offset):
    size = lax.axis_size(axis)
    return lax.ppermute(block, axis, [(i, (i + offset) % size) for i in range(size)])


def on_device(queries, past_cache, lengths, live_counts, adapter_index, adapter_down, adapter_up):
    slots, cols = queries.shape
    heads = cols // HEAD_DIM
    replicas = lax.axis_size("replica")
    tensor = lax.axis_size("tensor")
    pad = 16
    while pad < slots or pad * replicas % LANES:
        pad *= 2
    base = (lax.axis_index("replica") * adapter_down.shape[0]).astype(jnp.int32).reshape(1)
    rows = attend(queries, past_cache, lengths, live_counts, adapter_index)
    gathered = [rows] + [shift(rows, "replica", k) for k in range(1, replicas)]
    attention = unfold(rows, slots, heads)
    partial, index = lower(base, adapter_down, gathered, slots, heads, pad)
    partials = [partial] + [shift(partial, "tensor", k) for k in range(1, tensor)]
    widened = raise_rows(base, index, adapter_up, partials, slots, heads, pad, replicas)
    returned = [widened[0]] + [shift(widened[k], "replica", -k) for k in range(1, replicas)]
    adapted = merge(returned, slots, heads)
    return (attention, adapted)


def solution(mesh):
    in_specs = (
        P(("groups", "replica"), "tensor"),
        P(None, ("groups", "replica"), None, "tensor"),
        P(("groups", "replica")),
        P(("groups", "replica")),
        P(("groups", "replica")),
        P("replica", None, "tensor"),
        P("replica", None, "tensor"),
    )
    out_specs = (P(("groups", "replica"), "tensor"), P(("groups", "replica"), "tensor"))
    return jax.shard_map(
        on_device, mesh=mesh, in_specs=in_specs, out_specs=out_specs, check_vma=False
    )
```

```python
import functools
import math

import jax
import jax.numpy as jnp
from jax import lax
from jax.experimental import pallas as pl
from jax.experimental.pallas import tpu as pltpu
from jax.sharding import PartitionSpec as P

HEAD_DIM = 128
STAY = 16
SCALING = 2.0
LANES = 128
DIGIT = 7

VMEM = pl.BlockSpec(memory_space=pltpu.VMEM)
SMEM = pl.BlockSpec(memory_space=pltpu.SMEM)
HBM = pl.BlockSpec(memory_space=pltpu.HBM)
PARAMS = pltpu.CompilerParams(vmem_limit_bytes=16 * 2**20)


def chunks_of(slots):
    for parts in (3, 4, 2):
        if slots % parts == 0:
            return parts
    return 1


def attend_kernel(
    q_ref, cache_ref, lengths_ref, index_ref, rows_ref,
    q_flat, lengths, index, keys, values, q_rows, o_rows, small, large,
):
    slots, cols = q_ref.shape
    heads = cols // HEAD_DIM
    context, width = keys.shape[1:]
    key_heads = width // HEAD_DIM
    group = heads // key_heads
    parts = chunks_of(slots)
    step = slots // parts
    fetches = []
    for number, (source, target) in enumerate(((q_ref, q_flat), (lengths_ref, lengths), (index_ref, index))):
        fetches.append(pltpu.make_async_copy(source, target, small.at[number]))
        fetches[-1].start()
    copies = []
    for side, buffer in enumerate((keys, values)):
        for part in range(parts):
            span = pl.ds(part * step, step)
            copies.append(pltpu.make_async_copy(cache_ref.at[side, span], buffer.at[span], large.at[side, part]))
            copies[-1].start()
    for fetch in fetches:
        fetch.wait()
    for head in range(heads):
        block = q_flat[:, head * HEAD_DIM : (head + 1) * HEAD_DIM]
        q_rows[pl.ds(head, slots, stride=heads), :] = block.astype(jnp.float32)
    owner = lax.broadcasted_iota(jnp.int32, (heads, HEAD_DIM), 0) // group
    position = lax.broadcasted_iota(jnp.int32, (heads, context), 1)
    weights = []
    for slot in range(slots):
        if slot % step == 0:
            copies[slot // step].wait()
        rows = q_rows[slot * heads : (slot + 1) * heads, :]
        wide = [jnp.where(owner == k, rows, 0.0) for k in range(key_heads)]
        wide = jnp.concatenate(wide, axis=1).astype(jnp.bfloat16)
        scores = lax.dot_general(
            wide, keys[slot], (((1,), (1,)), ((), ())), preferred_element_type=jnp.float32
        ) / math.sqrt(HEAD_DIM)
        scores = jnp.where(position < lengths[slot], scores, -jnp.inf)
        raised = jnp.exp(scores - jnp.max(scores, axis=-1, keepdims=True))
        weights.append((raised / jnp.sum(raised, axis=-1, keepdims=True)).astype(jnp.bfloat16))
    for slot in range(slots):
        if slot % step == 0:
            copies[parts + slot // step].wait()
        mixed = jnp.dot(weights[slot], values[slot], preferred_element_type=jnp.float32)
        rows = mixed[:, :HEAD_DIM]
        for k in range(1, key_heads):
            rows = jnp.where(owner == k, mixed[:, k * HEAD_DIM : (k + 1) * HEAD_DIM], rows)
        o_rows[slot * heads : (slot + 1) * heads, :] = rows
    rows_ref[: slots * heads, :] = o_rows[...].astype(jnp.bfloat16)
    lane = lax.broadcasted_iota(jnp.int32, (16, LANES), 1)
    line = lax.broadcasted_iota(jnp.int32, (16, LANES), 0)
    named = jnp.zeros((16, LANES), jnp.int32)
    for slot in range(slots):
        named = jnp.where(lane == slot, index[slot], named)
    digits = jnp.where(line == 0, named >> DIGIT, named & ((1 << DIGIT) - 1))
    rows_ref[slots * heads :, :] = digits.astype(jnp.float32).astype(jnp.bfloat16)


def attend(queries, past_cache, lengths, adapter_index):
    slots, cols = queries.shape
    heads = cols // HEAD_DIM
    buffer = pltpu.VMEM(past_cache.shape[1:], past_cache.dtype)
    return pl.pallas_call(
        attend_kernel,
        out_shape=jax.ShapeDtypeStruct((slots * heads + 16, HEAD_DIM), jnp.bfloat16),
        in_specs=[HBM] * 4,
        out_specs=VMEM,
        scratch_shapes=[
            pltpu.VMEM(queries.shape, queries.dtype),
            pltpu.SMEM(lengths.shape, jnp.int32),
            pltpu.SMEM(adapter_index.shape, jnp.int32),
            buffer,
            buffer,
            pltpu.VMEM((slots * heads, HEAD_DIM), jnp.float32),
            pltpu.VMEM((slots * heads, HEAD_DIM), jnp.float32),
            pltpu.SemaphoreType.DMA((3,)),
            pltpu.SemaphoreType.DMA((2, chunks_of(slots))),
        ],
        cost_estimate=pl.CostEstimate(
            flops=4 * past_cache.size * heads, bytes_accessed=2 * past_cache.size, transcendentals=0
        ),
        compiler_params=PARAMS,
        name="attend",
    )(*[pltpu.with_memory_space_constraint(x, pltpu.HBM) for x in (queries, past_cache, lengths, adapter_index)])


def alive_lines(live_ref, slots):
    slot = lax.broadcasted_iota(jnp.int32, (slots, HEAD_DIM), 0)
    return (slot >= STAY) | (slot < live_ref[0])


def attention_kernel(slots, heads, live_ref, rows_ref, out_ref, alive_ref, flat):
    alive = alive_lines(live_ref, slots)
    alive_ref[...] = alive.astype(jnp.float32)
    flat[...] = rows_ref[: slots * heads, :].astype(jnp.float32)
    for head in range(heads):
        block = flat[pl.ds(head, slots, stride=heads), :]
        out_ref[:, head * HEAD_DIM : (head + 1) * HEAD_DIM] = jnp.where(alive, block, 0.0).astype(out_ref.dtype)


def attention_out(live, rows, slots, heads):
    return pl.pallas_call(
        functools.partial(attention_kernel, slots, heads),
        out_shape=(
            jax.ShapeDtypeStruct((slots, heads * HEAD_DIM), jnp.bfloat16),
            jax.ShapeDtypeStruct((slots, HEAD_DIM), jnp.float32),
        ),
        in_specs=[SMEM, VMEM],
        out_specs=(VMEM, VMEM),
        scratch_shapes=[pltpu.VMEM((slots * heads, HEAD_DIM), jnp.float32)],
        compiler_params=PARAMS,
        name="attention_out",
    )(live, rows)


def adapted_kernel(slots, heads, alive_ref, own_ref, *refs):
    rows_refs, out_ref, flat = refs[:-2], refs[-2], refs[-1]
    alive = alive_ref[...] > 0
    if rows_refs:
        total = rows_refs[0][...].astype(jnp.float32)
        for other in rows_refs[1:]:
            total += other[...].astype(jnp.float32)
        flat[...] = total
    for head in range(heads):
        block = own_ref[:, head * HEAD_DIM : (head + 1) * HEAD_DIM]
        if rows_refs:
            block += flat[pl.ds(head, slots, stride=heads), :]
        out_ref[:, head * HEAD_DIM : (head + 1) * HEAD_DIM] = jnp.where(alive, block, 0.0).astype(out_ref.dtype)


def adapted_out(alive, own, rows, slots, heads):
    return pl.pallas_call(
        functools.partial(adapted_kernel, slots, heads),
        out_shape=jax.ShapeDtypeStruct((slots, heads * HEAD_DIM), jnp.bfloat16),
        in_specs=[VMEM] * (2 + len(rows)),
        out_specs=VMEM,
        scratch_shapes=[pltpu.VMEM((slots * heads, HEAD_DIM), jnp.float32)],
        compiler_params=PARAMS,
        name="adapted_out",
    )(alive, own, *rows)


def first_adapter(holder, local_count):
    return (lax.axis_index("replica") ^ holder) * local_count


def lower_kernel(slots, heads, pad, sources, holders, before, *refs):
    down_refs, rows_refs = refs[:holders], refs[holders : holders + sources]
    partial_ref, index_ref, flat, wide = refs[-4:]
    local_count, rank, cols = down_refs[0].shape
    for source in range(sources):
        flat[source, : slots * heads, :] = rows_refs[source][: slots * heads, :].astype(jnp.float32)
        if pad > slots:
            flat[source, slots * heads :, :] = jnp.zeros(((pad - slots) * heads, HEAD_DIM), jnp.float32)
        digits = rows_refs[source][slots * heads :, :].astype(jnp.float32).astype(jnp.int32)
        index = (digits[0:1, :] << DIGIT) + digits[1:2, :]
        index_ref[:, source * pad : (source + 1) * pad] = index[:, :pad]
    for source in range(sources):
        for head in range(heads):
            wide[source * pad : (source + 1) * pad, head * HEAD_DIM : (head + 1) * HEAD_DIM] = flat[
                source, pl.ds(head, pad, stride=heads), :
            ].astype(jnp.bfloat16)
    total = jnp.zeros((rank, sources * pad), jnp.float32)
    for holder in range(holders):
        down = down_refs[holder][...].reshape(local_count * rank, cols)
        every = lax.dot_general(down, wide[...], (((1,), (1,)), ((), ())), preferred_element_type=jnp.float32)
        base = first_adapter(holder, local_count)
        for local in range(local_count):
            mine = index_ref[...] == base + local
            total += jnp.where(mine, every[local * rank : (local + 1) * rank, :], 0.0)
    if before:
        partial_ref[: before * rank, :] = refs[holders + sources][...]
    for source in range(sources):
        partial_ref[(before + source) * rank : (before + source + 1) * rank, :] = total[:, source * pad : (source + 1) * pad]


def lower(downs, rows, slots, heads, pad, name, cost, earlier=()):
    sources = len(rows)
    rank = downs[0].shape[1]
    before = sum(part.shape[0] // rank for part in earlier)
    return pl.pallas_call(
        functools.partial(lower_kernel, slots, heads, pad, sources, len(downs), before),
        out_shape=(
            jax.ShapeDtypeStruct(((before + sources) * rank, pad), jnp.float32),
            jax.ShapeDtypeStruct((1, sources * pad), jnp.int32),
        ),
        in_specs=[VMEM] * (len(downs) + sources + len(earlier)),
        out_specs=(VMEM, VMEM),
        scratch_shapes=[
            pltpu.VMEM((sources, pad * heads, HEAD_DIM), jnp.float32),
            pltpu.VMEM((sources * pad, heads * HEAD_DIM), jnp.bfloat16),
        ],
        cost_estimate=pl.CostEstimate(flops=cost, bytes_accessed=0, transcendentals=0),
        compiler_params=PARAMS,
        name=name,
    )(*downs, *rows, *earlier)


def spread_ranks(index, total, holders, local_count):
    total = SCALING * total
    high = total.astype(jnp.bfloat16).astype(jnp.float32)
    spread = []
    for part in (high, total - high):
        for holder in range(holders):
            for local in range(local_count):
                mine = index == first_adapter(holder, local_count) + local
                spread.append(jnp.where(mine, part, 0.0))
    return jnp.concatenate(spread, axis=0).astype(jnp.bfloat16)


def stack_ups(up_refs):
    local_count, rank, cols = up_refs[0].shape
    up = [up_ref[...].reshape(local_count * rank, cols) for up_ref in up_refs]
    return jnp.concatenate(up + up, axis=0)


def raise_kernel(slots, heads, pad, sources, holders, index_ref, *refs):
    up_refs, partials, outs, flat = refs[:holders], refs[holders : -sources - 1], refs[-sources - 1 : -1], refs[-1]
    local_count, rank, cols = up_refs[0].shape
    up = stack_ups(up_refs)
    for source in range(sources):
        lines = slice((1 + source) * rank, (2 + source) * rank)
        total = partials[0][lines, :]
        for other in partials[1:]:
            total += other[lines, :]
        spread = spread_ranks(index_ref[:, source * pad : (source + 1) * pad], total, holders, local_count)
        wide = lax.dot_general(spread, up, (((0,), (0,)), ((), ())), preferred_element_type=jnp.float32)
        for head in range(heads):
            flat[pl.ds(head, slots, stride=heads), :] = wide[:slots, head * HEAD_DIM : (head + 1) * HEAD_DIM]
        outs[source][...] = flat[...].astype(jnp.bfloat16)


def raise_rows(index, ups, partials, slots, heads, pad, sources):
    return pl.pallas_call(
        functools.partial(raise_kernel, slots, heads, pad, sources, len(ups)),
        out_shape=[jax.ShapeDtypeStruct((slots * heads, HEAD_DIM), jnp.bfloat16)] * sources,
        in_specs=[VMEM] * (1 + len(ups) + len(partials)),
        out_specs=[VMEM] * sources,
        scratch_shapes=[pltpu.VMEM((slots * heads, HEAD_DIM), jnp.float32)],
        compiler_params=PARAMS,
        name="raise_rows",
    )(index, *ups, *partials)


def raise_own_kernel(slots, holders, index_ref, *refs):
    up_refs, partials, out_ref = refs[:holders], refs[holders:-1], refs[-1]
    local_count, rank, cols = up_refs[0].shape
    total = partials[0][:rank, :]
    for other in partials[1:]:
        total += other[:rank, :]
    spread = spread_ranks(index_ref[...], total, holders, local_count)
    wide = lax.dot_general(spread, stack_ups(up_refs), (((0,), (0,)), ((), ())), preferred_element_type=jnp.float32)
    out_ref[...] = wide[:slots, :]


def raise_own(index, ups, partials, slots):
    return pl.pallas_call(
        functools.partial(raise_own_kernel, slots, len(ups)),
        out_shape=jax.ShapeDtypeStruct((slots, ups[0].shape[2]), jnp.float32),
        in_specs=[VMEM] * (1 + len(ups) + len(partials)),
        out_specs=VMEM,
        compiler_params=PARAMS,
        name="raise_own",
    )(index, *ups, *partials)


def shift(block, axis, offset):
    size = lax.axis_size(axis)
    return lax.ppermute(block, axis, [(i, (i + offset) % size) for i in range(size)])


def swap(block, axis):
    size = lax.axis_size(axis)
    return lax.ppermute(block, axis, [(i, i ^ 1) for i in range(size)])


def on_device(queries, past_cache, lengths, live_counts, adapter_index, adapter_down, adapter_up):
    slots, cols = queries.shape
    heads = cols // HEAD_DIM
    replicas = lax.axis_size("replica")
    tensor = lax.axis_size("tensor")
    holders = 2 if replicas % 2 == 0 else 1
    sources = replicas // holders
    pad = 16
    while pad < slots:
        pad *= 2
    downs = [adapter_down] + [swap(adapter_down, "replica") for _ in range(1, holders)]
    rows = attend(queries, past_cache, lengths, adapter_index)
    gathered = [shift(rows, "replica", holders * k) for k in range(1, sources)]
    attention, alive = attention_out(live_counts, rows, slots, heads)
    own_partial, own_index = lower(downs, [rows], slots, heads, pad, "lower_own", 10**6)
    later_up = lax.optimization_barrier((adapter_up, alive))[0]
    ups = [adapter_up] + [swap(later_up, "replica") for _ in range(1, holders)]
    partial, index = lower(downs, gathered, slots, heads, pad, "lower", 2 * 10**10, [own_partial])
    partials = [partial] + [shift(partial, "tensor", k) for k in range(1, tensor)]
    widened = raise_rows(index, ups, partials, slots, heads, pad, sources - 1)
    returned = [shift(widened[k - 1], "replica", -holders * k) for k in range(1, sources)]
    own = raise_own(own_index, ups, partials, slots)
    adapted = adapted_out(alive, own, returned, slots, heads)
    return (attention, adapted)


def solution(mesh):
    in_specs = (
        P(("groups", "replica"), "tensor"),
        P(None, ("groups", "replica"), None, "tensor"),
        P(("groups", "replica")),
        P(("groups", "replica")),
        P(("groups", "replica")),
        P("replica", None, "tensor"),
        P("replica", None, "tensor"),
    )
    out_specs = (P(("groups", "replica"), "tensor"), P(("groups", "replica"), "tensor"))
    return jax.shard_map(
        on_device, mesh=mesh, in_specs=in_specs, out_specs=out_specs, check_vma=False
    )
```

```python
import functools
import math

import jax
import jax.numpy as jnp
from jax import lax
from jax.experimental import pallas as pl
from jax.experimental.pallas import tpu as pltpu
from jax.sharding import PartitionSpec as P

HEAD_DIM = 128
STAY = 16
SCALING = 2.0
LANES = 128
DIGIT = 7

VMEM = pl.BlockSpec(memory_space=pltpu.VMEM)
SMEM = pl.BlockSpec(memory_space=pltpu.SMEM)
HBM = pl.BlockSpec(memory_space=pltpu.HBM)
PARAMS = pltpu.CompilerParams(vmem_limit_bytes=16 * 2**20)


def attend_kernel(
    q_ref, cache_ref, lengths_ref, index_ref, rows_ref,
    q_flat, lengths, index, keys, values, q_rows, o_rows, small, large,
):
    slots, cols = q_ref.shape
    heads = cols // HEAD_DIM
    context, width = keys.shape[1:]
    key_heads = width // HEAD_DIM
    group = heads // key_heads
    fetches = []
    for number, (source, target) in enumerate(((q_ref, q_flat), (lengths_ref, lengths), (index_ref, index))):
        fetches.append(pltpu.make_async_copy(source, target, small.at[number]))
        fetches[-1].start()
    copies = []
    for side, buffer in enumerate((keys, values)):
        copies.append(pltpu.make_async_copy(cache_ref.at[side], buffer, large.at[side]))
        copies[-1].start()
    for fetch in fetches:
        fetch.wait()
    for head in range(heads):
        block = q_flat[:, head * HEAD_DIM : (head + 1) * HEAD_DIM]
        q_rows[pl.ds(head, slots, stride=heads), :] = block.astype(jnp.float32)
    owner = lax.broadcasted_iota(jnp.int32, (heads, HEAD_DIM), 0) // group
    position = lax.broadcasted_iota(jnp.int32, (heads, context), 1)
    weights = []
    copies[0].wait()
    for slot in range(slots):
        rows = q_rows[slot * heads : (slot + 1) * heads, :]
        wide = [jnp.where(owner == k, rows, 0.0) for k in range(key_heads)]
        wide = jnp.concatenate(wide, axis=1).astype(jnp.bfloat16)
        scores = lax.dot_general(
            wide, keys[slot], (((1,), (1,)), ((), ())), preferred_element_type=jnp.float32
        ) / math.sqrt(HEAD_DIM)
        scores = jnp.where(position < lengths[slot], scores, -jnp.inf)
        raised = jnp.exp(scores - jnp.max(scores, axis=-1, keepdims=True))
        weights.append((raised / jnp.sum(raised, axis=-1, keepdims=True)).astype(jnp.bfloat16))
    copies[1].wait()
    for slot in range(slots):
        mixed = jnp.dot(weights[slot], values[slot], preferred_element_type=jnp.float32)
        rows = mixed[:, :HEAD_DIM]
        for k in range(1, key_heads):
            rows = jnp.where(owner == k, mixed[:, k * HEAD_DIM : (k + 1) * HEAD_DIM], rows)
        o_rows[slot * heads : (slot + 1) * heads, :] = rows
    rows_ref[: slots * heads, :] = o_rows[...].astype(jnp.bfloat16)
    lane = lax.broadcasted_iota(jnp.int32, (16, LANES), 1)
    line = lax.broadcasted_iota(jnp.int32, (16, LANES), 0)
    named = jnp.zeros((16, LANES), jnp.int32)
    for slot in range(slots):
        named = jnp.where(lane == slot, index[slot], named)
    digits = jnp.where(line == 0, named >> DIGIT, named & ((1 << DIGIT) - 1))
    rows_ref[slots * heads :, :] = digits.astype(jnp.float32).astype(jnp.bfloat16)


def attend(queries, past_cache, lengths, adapter_index):
    slots, cols = queries.shape
    heads = cols // HEAD_DIM
    buffer = pltpu.VMEM(past_cache.shape[1:], past_cache.dtype)
    return pl.pallas_call(
        attend_kernel,
        out_shape=jax.ShapeDtypeStruct((slots * heads + 16, HEAD_DIM), jnp.bfloat16),
        in_specs=[HBM] * 4,
        out_specs=VMEM,
        scratch_shapes=[
            pltpu.VMEM(queries.shape, queries.dtype),
            pltpu.SMEM(lengths.shape, jnp.int32),
            pltpu.SMEM(adapter_index.shape, jnp.int32),
            buffer,
            buffer,
            pltpu.VMEM((slots * heads, HEAD_DIM), jnp.float32),
            pltpu.VMEM((slots * heads, HEAD_DIM), jnp.float32),
            pltpu.SemaphoreType.DMA((3,)),
            pltpu.SemaphoreType.DMA((2,)),
        ],
        cost_estimate=pl.CostEstimate(
            flops=4 * past_cache.size * heads, bytes_accessed=2 * past_cache.size, transcendentals=0
        ),
        compiler_params=PARAMS,
        name="attend",
    )(*[pltpu.with_memory_space_constraint(x, pltpu.HBM) for x in (queries, past_cache, lengths, adapter_index)])


def alive_lines(live_ref, slots):
    slot = lax.broadcasted_iota(jnp.int32, (slots, HEAD_DIM), 0)
    return (slot >= STAY) | (slot < live_ref[0])


def attention_kernel(slots, heads, live_ref, rows_ref, out_ref, alive_ref, flat):
    alive = alive_lines(live_ref, slots)
    alive_ref[...] = alive.astype(jnp.float32)
    flat[...] = rows_ref[: slots * heads, :].astype(jnp.float32)
    for head in range(heads):
        block = flat[pl.ds(head, slots, stride=heads), :]
        out_ref[:, head * HEAD_DIM : (head + 1) * HEAD_DIM] = jnp.where(alive, block, 0.0).astype(out_ref.dtype)


def attention_out(live, rows, slots, heads):
    return pl.pallas_call(
        functools.partial(attention_kernel, slots, heads),
        out_shape=(
            jax.ShapeDtypeStruct((slots, heads * HEAD_DIM), jnp.bfloat16),
            jax.ShapeDtypeStruct((slots, HEAD_DIM), jnp.float32),
        ),
        in_specs=[SMEM, VMEM],
        out_specs=(VMEM, VMEM),
        scratch_shapes=[pltpu.VMEM((slots * heads, HEAD_DIM), jnp.float32)],
        compiler_params=PARAMS,
        name="attention_out",
    )(live, rows)


def adapted_kernel(slots, heads, alive_ref, own_ref, *refs):
    rows_refs, out_ref, flat = refs[:-2], refs[-2], refs[-1]
    alive = alive_ref[...] > 0
    if rows_refs:
        total = rows_refs[0][...].astype(jnp.float32)
        for other in rows_refs[1:]:
            total += other[...].astype(jnp.float32)
        flat[...] = total
    for head in range(heads):
        block = own_ref[:, head * HEAD_DIM : (head + 1) * HEAD_DIM]
        if rows_refs:
            block += flat[pl.ds(head, slots, stride=heads), :]
        out_ref[:, head * HEAD_DIM : (head + 1) * HEAD_DIM] = jnp.where(alive, block, 0.0).astype(out_ref.dtype)


def adapted_out(alive, own, rows, slots, heads):
    return pl.pallas_call(
        functools.partial(adapted_kernel, slots, heads),
        out_shape=jax.ShapeDtypeStruct((slots, heads * HEAD_DIM), jnp.bfloat16),
        in_specs=[VMEM] * (2 + len(rows)),
        out_specs=VMEM,
        scratch_shapes=[pltpu.VMEM((slots * heads, HEAD_DIM), jnp.float32)],
        compiler_params=PARAMS,
        name="adapted_out",
    )(alive, own, *rows)


def first_adapter(holder, local_count):
    return (lax.axis_index("replica") ^ holder) * local_count


def unfold_rows(rows_ref, slots, heads, pad, flat, wide_ref, first):
    flat[: slots * heads, :] = rows_ref[: slots * heads, :].astype(jnp.float32)
    if pad > slots:
        flat[slots * heads :, :] = jnp.zeros(((pad - slots) * heads, HEAD_DIM), jnp.float32)
    for head in range(heads):
        wide_ref[first : first + pad, head * HEAD_DIM : (head + 1) * HEAD_DIM] = flat[
            pl.ds(head, pad, stride=heads), :
        ].astype(jnp.bfloat16)
    digits = rows_ref[slots * heads :, :].astype(jnp.float32).astype(jnp.int32)
    return ((digits[0:1, :] << DIGIT) + digits[1:2, :])[:, :pad]


def rank_rows(down_ref, holder, wide, named):
    local_count, rank, cols = down_ref.shape
    down = down_ref[...].reshape(local_count * rank, cols)
    every = lax.dot_general(down, wide, (((1,), (1,)), ((), ())), preferred_element_type=jnp.float32)
    base = first_adapter(holder, local_count)
    total = jnp.zeros((rank, named.shape[1]), jnp.float32)
    for local in range(local_count):
        total += jnp.where(named == base + local, every[local * rank : (local + 1) * rank, :], 0.0)
    return total


def lower_own_kernel(slots, heads, pad, down_ref, rows_ref, partial_ref, index_ref, wide_ref, flat):
    named = unfold_rows(rows_ref, slots, heads, pad, flat, wide_ref, 0)
    index_ref[...] = named
    partial_ref[...] = rank_rows(down_ref, 0, wide_ref[...], named)


def lower_own(down, rows, slots, heads, pad):
    rank = down.shape[1]
    return pl.pallas_call(
        functools.partial(lower_own_kernel, slots, heads, pad),
        out_shape=(
            jax.ShapeDtypeStruct((rank, pad), jnp.float32),
            jax.ShapeDtypeStruct((1, pad), jnp.int32),
            jax.ShapeDtypeStruct((pad, heads * HEAD_DIM), jnp.bfloat16),
        ),
        in_specs=[VMEM] * 2,
        out_specs=[VMEM] * 3,
        scratch_shapes=[pltpu.VMEM((pad * heads, HEAD_DIM), jnp.float32)],
        compiler_params=PARAMS,
        name="lower_own",
    )(down, rows)


def lower_kernel(slots, heads, pad, sources, holders, *refs):
    own_partial, own_index, own_wide = refs[:3]
    down_refs, rows_refs = refs[3 : 3 + holders], refs[3 + holders : 3 + holders + sources]
    partial_ref, index_ref, flat, wide = refs[-4:]
    rank = down_refs[0].shape[1]
    named = [own_index[...]]
    for source in range(sources):
        named.append(unfold_rows(rows_refs[source], slots, heads, pad, flat, wide, source * pad))
    for block in range(sources + 1):
        index_ref[block : block + 1, :] = named[block]
    total = own_partial[...]
    for holder in range(1, holders):
        total += rank_rows(down_refs[holder], holder, own_wide[...], named[0])
    totals = [total]
    for source in range(sources):
        total = jnp.zeros((rank, pad), jnp.float32)
        for holder in range(holders):
            total += rank_rows(down_refs[holder], holder, wide[source * pad : (source + 1) * pad, :], named[1 + source])
        totals.append(total)
    partial_ref[...] = jnp.concatenate(totals[1:] + totals[:1], axis=1)

def lower(own, downs, rows, slots, heads, pad):
    sources = len(rows)
    rank = downs[0].shape[1]
    return pl.pallas_call(
        functools.partial(lower_kernel, slots, heads, pad, sources, len(downs)),
        out_shape=(
            jax.ShapeDtypeStruct((rank, (1 + sources) * pad), jnp.float32),
            jax.ShapeDtypeStruct((1 + sources, pad), jnp.int32),
        ),
        in_specs=[VMEM] * (3 + len(downs) + sources),
        out_specs=[VMEM] * 2,
        scratch_shapes=[
            pltpu.VMEM((pad * heads, HEAD_DIM), jnp.float32),
            pltpu.VMEM((sources * pad, heads * HEAD_DIM), jnp.bfloat16),
        ],
        cost_estimate=pl.CostEstimate(flops=2 * 10**10, bytes_accessed=0, transcendentals=0),
        compiler_params=PARAMS,
        name="lower",
    )(*own, *downs, *rows)


def spread_ranks(index, total, holders, local_count):
    total = SCALING * total
    spread = []
    for holder in range(holders):
        for local in range(local_count):
            mine = index == first_adapter(holder, local_count) + local
            spread.append(jnp.where(mine, total, 0.0))
    return jnp.concatenate(spread, axis=0).astype(jnp.bfloat16)


def stack_ups(up_refs):
    local_count, rank, cols = up_refs[0].shape
    up = [up_ref[...].reshape(local_count * rank, cols) for up_ref in up_refs]
    return jnp.concatenate(up, axis=0)


def raise_kernel(slots, heads, sources, holders, index_ref, *refs):
    up_refs, partials, outs, flat = refs[:holders], refs[holders : -sources - 1], refs[-sources - 1 : -1], refs[-1]
    local_count, rank, cols = up_refs[0].shape
    up = stack_ups(up_refs)
    packed = partials[0][...]
    for other in partials[1:]:
        packed += other[...]
    pad = index_ref.shape[1]
    for source in range(sources):
        total = packed[:, source * pad : (source + 1) * pad]
        spread = spread_ranks(index_ref[1 + source : 2 + source, :], total, holders, local_count)
        wide = lax.dot_general(spread, up, (((0,), (0,)), ((), ())), preferred_element_type=jnp.float32)
        for head in range(heads):
            flat[pl.ds(head, slots, stride=heads), :] = wide[:slots, head * HEAD_DIM : (head + 1) * HEAD_DIM]
        outs[source][...] = flat[...].astype(jnp.bfloat16)


def raise_rows(index, ups, partials, slots, heads, sources):
    return pl.pallas_call(
        functools.partial(raise_kernel, slots, heads, sources, len(ups)),
        out_shape=[jax.ShapeDtypeStruct((slots * heads, HEAD_DIM), jnp.bfloat16)] * sources,
        in_specs=[VMEM] * (1 + len(ups) + len(partials)),
        out_specs=[VMEM] * sources,
        scratch_shapes=[pltpu.VMEM((slots * heads, HEAD_DIM), jnp.float32)],
        compiler_params=PARAMS,
        name="raise_rows",
    )(index, *ups, *partials)


def raise_own_kernel(slots, holders, index_ref, *refs):
    up_refs, partials, out_ref = refs[:holders], refs[holders:-1], refs[-1]
    local_count, rank, cols = up_refs[0].shape
    packed = partials[0][...]
    for other in partials[1:]:
        packed += other[...]
    total = packed[:, packed.shape[1] - index_ref.shape[1] :]
    spread = spread_ranks(index_ref[0:1, :], total, holders, local_count)
    wide = lax.dot_general(spread, stack_ups(up_refs), (((0,), (0,)), ((), ())), preferred_element_type=jnp.float32)
    out_ref[...] = wide[:slots, :]


def raise_own(index, ups, partials, slots):
    return pl.pallas_call(
        functools.partial(raise_own_kernel, slots, len(ups)),
        out_shape=jax.ShapeDtypeStruct((slots, ups[0].shape[2]), jnp.float32),
        in_specs=[VMEM] * (1 + len(ups) + len(partials)),
        out_specs=VMEM,
        compiler_params=PARAMS,
        name="raise_own",
    )(index, *ups, *partials)


def shift(block, axis, offset):
    size = lax.axis_size(axis)
    return lax.ppermute(block, axis, [(i, (i + offset) % size) for i in range(size)])


def swap(block, axis, bits=1):
    size = lax.axis_size(axis)
    return lax.ppermute(block, axis, [(i, i ^ bits) for i in range(size)])


def exchange(block, axis):
    size = lax.axis_size(axis)
    if size & (size - 1):
        return [shift(block, axis, k) for k in range(1, size)]
    return [swap(block, axis, k) for k in [*range(2, size), 1]]


def on_device(queries, past_cache, lengths, live_counts, adapter_index, adapter_down, adapter_up):
    slots, cols = queries.shape
    heads = cols // HEAD_DIM
    replicas = lax.axis_size("replica")
    holders = 2 if replicas % 2 == 0 else 1
    sources = replicas // holders
    pad = 16
    while pad < slots:
        pad *= 2
    downs = [adapter_down] + [swap(adapter_down, "replica") for _ in range(1, holders)]
    rows = attend(queries, past_cache, lengths, adapter_index)
    gathered = [shift(rows, "replica", holders * k) for k in range(1, sources)]
    attention, alive = attention_out(live_counts, rows, slots, heads)
    own = lower_own(adapter_down, rows, slots, heads, pad)
    later_up = lax.optimization_barrier((adapter_up, alive, own[0]))[0]
    ups = [adapter_up] + [swap(later_up, "replica") for _ in range(1, holders)]
    partial, index = lower(own, downs, gathered, slots, heads, pad)
    partials = [partial] + exchange(partial, "tensor")
    widened = raise_rows(index, ups, partials, slots, heads, sources - 1)
    returned = [shift(widened[k - 1], "replica", -holders * k) for k in range(1, sources)]
    own = raise_own(index, ups, partials, slots)
    adapted = adapted_out(alive, own, returned, slots, heads)
    return (attention, adapted)


def solution(mesh):
    in_specs = (
        P(("groups", "replica"), "tensor"),
        P(None, ("groups", "replica"), None, "tensor"),
        P(("groups", "replica")),
        P(("groups", "replica")),
        P(("groups", "replica")),
        P("replica", None, "tensor"),
        P("replica", None, "tensor"),
    )
    out_specs = (P(("groups", "replica"), "tensor"), P(("groups", "replica"), "tensor"))
    return jax.shard_map(
        on_device, mesh=mesh, in_specs=in_specs, out_specs=out_specs, check_vma=False
    )
```

```python
import functools
import math

import jax
import jax.numpy as jnp
from jax import lax
from jax.experimental import pallas as pl
from jax.experimental.pallas import tpu as pltpu
from jax.sharding import PartitionSpec as P

HEAD_DIM = 128
STAY = 16
SCALING = 2.0
LANES = 128
DIGIT = 7

VMEM = pl.BlockSpec(memory_space=pltpu.VMEM)
SMEM = pl.BlockSpec(memory_space=pltpu.SMEM)
HBM = pl.BlockSpec(memory_space=pltpu.HBM)
PARAMS = pltpu.CompilerParams(vmem_limit_bytes=16 * 2**20)


def attend_kernel(
    q_ref, cache_ref, lengths_ref, index_ref, rows_ref,
    q_flat, lengths, index, keys, values, q_rows, o_rows, small, large,
):
    slots, cols = q_ref.shape
    heads = cols // HEAD_DIM
    context, width = keys.shape[1:]
    key_heads = width // HEAD_DIM
    group = heads // key_heads
    fetches = []
    for number, (source, target) in enumerate(((q_ref, q_flat), (lengths_ref, lengths), (index_ref, index))):
        fetches.append(pltpu.make_async_copy(source, target, small.at[number]))
        fetches[-1].start()
    copies = []
    for side, buffer in enumerate((keys, values)):
        copies.append(pltpu.make_async_copy(cache_ref.at[side], buffer, large.at[side]))
        copies[-1].start()
    for fetch in fetches:
        fetch.wait()
    for head in range(heads):
        block = q_flat[:, head * HEAD_DIM : (head + 1) * HEAD_DIM]
        q_rows[pl.ds(head, slots, stride=heads), :] = block.astype(jnp.float32)
    owner = lax.broadcasted_iota(jnp.int32, (heads, HEAD_DIM), 0) // group
    position = lax.broadcasted_iota(jnp.int32, (heads, context), 1)
    weights = []
    copies[0].wait()
    for slot in range(slots):
        rows = q_rows[slot * heads : (slot + 1) * heads, :]
        wide = [jnp.where(owner == k, rows, 0.0) for k in range(key_heads)]
        wide = jnp.concatenate(wide, axis=1).astype(jnp.bfloat16)
        scores = lax.dot_general(
            wide, keys[slot], (((1,), (1,)), ((), ())), preferred_element_type=jnp.float32
        ) / math.sqrt(HEAD_DIM)
        scores = jnp.where(position < lengths[slot], scores, -jnp.inf)
        raised = jnp.exp(scores - jnp.max(scores, axis=-1, keepdims=True))
        weights.append((raised / jnp.sum(raised, axis=-1, keepdims=True)).astype(jnp.bfloat16))
    copies[1].wait()
    for slot in range(slots):
        mixed = jnp.dot(weights[slot], values[slot], preferred_element_type=jnp.float32)
        rows = mixed[:, :HEAD_DIM]
        for k in range(1, key_heads):
            rows = jnp.where(owner == k, mixed[:, k * HEAD_DIM : (k + 1) * HEAD_DIM], rows)
        o_rows[slot * heads : (slot + 1) * heads, :] = rows
    rows_ref[: slots * heads, :] = o_rows[...].astype(jnp.bfloat16)
    lane = lax.broadcasted_iota(jnp.int32, (16, LANES), 1)
    line = lax.broadcasted_iota(jnp.int32, (16, LANES), 0)
    named = jnp.zeros((16, LANES), jnp.int32)
    for slot in range(slots):
        named = jnp.where(lane == slot, index[slot], named)
    digits = jnp.where(line == 0, named >> DIGIT, named & ((1 << DIGIT) - 1))
    rows_ref[slots * heads :, :] = digits.astype(jnp.float32).astype(jnp.bfloat16)


def attend(queries, past_cache, lengths, adapter_index):
    slots, cols = queries.shape
    heads = cols // HEAD_DIM
    buffer = pltpu.VMEM(past_cache.shape[1:], past_cache.dtype)
    return pl.pallas_call(
        attend_kernel,
        out_shape=jax.ShapeDtypeStruct((slots * heads + 16, HEAD_DIM), jnp.bfloat16),
        in_specs=[HBM] * 4,
        out_specs=VMEM,
        scratch_shapes=[
            pltpu.VMEM(queries.shape, queries.dtype),
            pltpu.SMEM(lengths.shape, jnp.int32),
            pltpu.SMEM(adapter_index.shape, jnp.int32),
            buffer,
            buffer,
            pltpu.VMEM((slots * heads, HEAD_DIM), jnp.float32),
            pltpu.VMEM((slots * heads, HEAD_DIM), jnp.float32),
            pltpu.SemaphoreType.DMA((3,)),
            pltpu.SemaphoreType.DMA((2,)),
        ],
        cost_estimate=pl.CostEstimate(
            flops=4 * past_cache.size * heads, bytes_accessed=2 * past_cache.size, transcendentals=0
        ),
        compiler_params=PARAMS,
        name="attend",
    )(*[pltpu.with_memory_space_constraint(x, pltpu.HBM) for x in (queries, past_cache, lengths, adapter_index)])


def alive_lines(live_ref, slots):
    slot = lax.broadcasted_iota(jnp.int32, (slots, HEAD_DIM), 0)
    return (slot >= STAY) | (slot < live_ref[0])


def attention_kernel(slots, heads, live_ref, rows_ref, out_ref, alive_ref, flat):
    alive = alive_lines(live_ref, slots)
    alive_ref[...] = alive.astype(jnp.float32)
    flat[...] = rows_ref[: slots * heads, :].astype(jnp.float32)
    for head in range(heads):
        block = flat[pl.ds(head, slots, stride=heads), :]
        out_ref[:, head * HEAD_DIM : (head + 1) * HEAD_DIM] = jnp.where(alive, block, 0.0).astype(out_ref.dtype)


def attention_out(live, rows, slots, heads):
    return pl.pallas_call(
        functools.partial(attention_kernel, slots, heads),
        out_shape=(
            jax.ShapeDtypeStruct((slots, heads * HEAD_DIM), jnp.bfloat16),
            jax.ShapeDtypeStruct((slots, HEAD_DIM), jnp.float32),
        ),
        in_specs=[SMEM, VMEM],
        out_specs=(VMEM, VMEM),
        scratch_shapes=[pltpu.VMEM((slots * heads, HEAD_DIM), jnp.float32)],
        compiler_params=PARAMS,
        name="attention_out",
    )(live, rows)


def adapted_kernel(slots, heads, alive_ref, own_ref, *refs):
    rows_refs, out_ref, flat = refs[:-2], refs[-2], refs[-1]
    alive = alive_ref[...] > 0
    if rows_refs:
        total = rows_refs[0][...].astype(jnp.float32)
        for other in rows_refs[1:]:
            total += other[...].astype(jnp.float32)
        flat[...] = total
    for head in range(heads):
        block = own_ref[:, head * HEAD_DIM : (head + 1) * HEAD_DIM]
        if rows_refs:
            block += flat[pl.ds(head, slots, stride=heads), :]
        out_ref[:, head * HEAD_DIM : (head + 1) * HEAD_DIM] = jnp.where(alive, block, 0.0).astype(out_ref.dtype)


def adapted_out(alive, own, rows, slots, heads):
    return pl.pallas_call(
        functools.partial(adapted_kernel, slots, heads),
        out_shape=jax.ShapeDtypeStruct((slots, heads * HEAD_DIM), jnp.bfloat16),
        in_specs=[VMEM] * (2 + len(rows)),
        out_specs=VMEM,
        scratch_shapes=[pltpu.VMEM((slots * heads, HEAD_DIM), jnp.float32)],
        compiler_params=PARAMS,
        name="adapted_out",
    )(alive, own, *rows)


def first_adapter(holder, local_count):
    return (lax.axis_index("replica") ^ holder) * local_count


def unfold_rows(rows_ref, slots, heads, pad, flat, wide_ref, first):
    flat[: slots * heads, :] = rows_ref[: slots * heads, :].astype(jnp.float32)
    if pad > slots:
        flat[slots * heads :, :] = jnp.zeros(((pad - slots) * heads, HEAD_DIM), jnp.float32)
    for head in range(heads):
        wide_ref[first : first + pad, head * HEAD_DIM : (head + 1) * HEAD_DIM] = flat[
            pl.ds(head, pad, stride=heads), :
        ].astype(jnp.bfloat16)
    digits = rows_ref[slots * heads :, :].astype(jnp.float32).astype(jnp.int32)
    return ((digits[0:1, :] << DIGIT) + digits[1:2, :])[:, :pad]


def rank_rows(down_ref, holder, wide, named):
    local_count, rank, cols = down_ref.shape
    down = down_ref[...].reshape(local_count * rank, cols)
    every = lax.dot_general(down, wide, (((1,), (1,)), ((), ())), preferred_element_type=jnp.float32)
    base = first_adapter(holder, local_count)
    total = jnp.zeros((rank, named.shape[1]), jnp.float32)
    for local in range(local_count):
        total += jnp.where(named == base + local, every[local * rank : (local + 1) * rank, :], 0.0)
    return total


def lower_own_kernel(slots, heads, pad, down_ref, rows_ref, partial_ref, index_ref, wide_ref, flat):
    named = unfold_rows(rows_ref, slots, heads, pad, flat, wide_ref, 0)
    index_ref[...] = named
    partial_ref[...] = rank_rows(down_ref, 0, wide_ref[...], named)


def lower_own(down, rows, slots, heads, pad):
    rank = down.shape[1]
    return pl.pallas_call(
        functools.partial(lower_own_kernel, slots, heads, pad),
        out_shape=(
            jax.ShapeDtypeStruct((rank, pad), jnp.float32),
            jax.ShapeDtypeStruct((1, pad), jnp.int32),
            jax.ShapeDtypeStruct((pad, heads * HEAD_DIM), jnp.bfloat16),
        ),
        in_specs=[VMEM] * 2,
        out_specs=[VMEM] * 3,
        scratch_shapes=[pltpu.VMEM((pad * heads, HEAD_DIM), jnp.float32)],
        compiler_params=PARAMS,
        name="lower_own",
    )(down, rows)


def lower_kernel(slots, heads, pad, sources, holders, *refs):
    own_partial, own_index, own_wide = refs[:3]
    down_refs, rows_refs = refs[3 : 3 + holders], refs[3 + holders : 3 + holders + sources]
    partial_ref, index_ref, flat, wide = refs[-4:]
    rank = down_refs[0].shape[1]
    named = [own_index[...]]
    for source in range(sources):
        named.append(unfold_rows(rows_refs[source], slots, heads, pad, flat, wide, source * pad))
    for block in range(sources + 1):
        index_ref[block : block + 1, :] = named[block]
    total = own_partial[...]
    for holder in range(1, holders):
        total += rank_rows(down_refs[holder], holder, own_wide[...], named[0])
    totals = [total]
    for source in range(sources):
        total = jnp.zeros((rank, pad), jnp.float32)
        for holder in range(holders):
            total += rank_rows(down_refs[holder], holder, wide[source * pad : (source + 1) * pad, :], named[1 + source])
        totals.append(total)
    partial_ref[...] = jnp.concatenate(totals[1:] + totals[:1], axis=1)

def lower(own, downs, rows, slots, heads, pad):
    sources = len(rows)
    rank = downs[0].shape[1]
    return pl.pallas_call(
        functools.partial(lower_kernel, slots, heads, pad, sources, len(downs)),
        out_shape=(
            jax.ShapeDtypeStruct((rank, (1 + sources) * pad), jnp.float32),
            jax.ShapeDtypeStruct((1 + sources, pad), jnp.int32),
        ),
        in_specs=[VMEM] * (3 + len(downs) + sources),
        out_specs=[VMEM] * 2,
        scratch_shapes=[
            pltpu.VMEM((pad * heads, HEAD_DIM), jnp.float32),
            pltpu.VMEM((sources * pad, heads * HEAD_DIM), jnp.bfloat16),
        ],
        cost_estimate=pl.CostEstimate(flops=2 * 10**10, bytes_accessed=0, transcendentals=0),
        compiler_params=PARAMS,
        name="lower",
    )(*own, *downs, *rows)


def spread_ranks(index, total, holders, local_count):
    total = SCALING * total
    spread = []
    for holder in range(holders):
        for local in range(local_count):
            mine = index == first_adapter(holder, local_count) + local
            spread.append(jnp.where(mine, total, 0.0))
    return jnp.concatenate(spread, axis=0).astype(jnp.bfloat16)


def stack_ups(up_refs):
    local_count, rank, cols = up_refs[0].shape
    up = [up_ref[...].reshape(local_count * rank, cols) for up_ref in up_refs]
    return jnp.concatenate(up, axis=0)


def raise_kernel(slots, heads, sources, holders, index_ref, *refs):
    up_refs, partials, outs, flat = refs[:holders], refs[holders : -sources - 1], refs[-sources - 1 : -1], refs[-1]
    local_count, rank, cols = up_refs[0].shape
    up = stack_ups(up_refs)
    packed = partials[0][...]
    for other in partials[1:]:
        packed += other[...]
    pad = index_ref.shape[1]
    for source in range(sources):
        total = packed[:, source * pad : (source + 1) * pad]
        spread = spread_ranks(index_ref[1 + source : 2 + source, :], total, holders, local_count)
        wide = lax.dot_general(spread, up, (((0,), (0,)), ((), ())), preferred_element_type=jnp.float32)
        for head in range(heads):
            flat[pl.ds(head, slots, stride=heads), :] = wide[:slots, head * HEAD_DIM : (head + 1) * HEAD_DIM]
        outs[source][...] = flat[...].astype(jnp.bfloat16)


def raise_rows(index, ups, partials, slots, heads, sources):
    return pl.pallas_call(
        functools.partial(raise_kernel, slots, heads, sources, len(ups)),
        out_shape=[jax.ShapeDtypeStruct((slots * heads, HEAD_DIM), jnp.bfloat16)] * sources,
        in_specs=[VMEM] * (1 + len(ups) + len(partials)),
        out_specs=[VMEM] * sources,
        scratch_shapes=[pltpu.VMEM((slots * heads, HEAD_DIM), jnp.float32)],
        compiler_params=PARAMS,
        name="raise_rows",
    )(index, *ups, *partials)


def raise_own_kernel(slots, holders, index_ref, *refs):
    up_refs, partials, out_ref = refs[:holders], refs[holders:-1], refs[-1]
    local_count, rank, cols = up_refs[0].shape
    packed = partials[0][...]
    for other in partials[1:]:
        packed += other[...]
    total = packed[:, packed.shape[1] - index_ref.shape[1] :]
    spread = spread_ranks(index_ref[0:1, :], total, holders, local_count)
    wide = lax.dot_general(spread, stack_ups(up_refs), (((0,), (0,)), ((), ())), preferred_element_type=jnp.float32)
    out_ref[...] = wide[:slots, :]


def raise_own(index, ups, partials, slots):
    return pl.pallas_call(
        functools.partial(raise_own_kernel, slots, len(ups)),
        out_shape=jax.ShapeDtypeStruct((slots, ups[0].shape[2]), jnp.float32),
        in_specs=[VMEM] * (1 + len(ups) + len(partials)),
        out_specs=VMEM,
        compiler_params=PARAMS,
        name="raise_own",
    )(index, *ups, *partials)


def shift(block, axis, offset):
    size = lax.axis_size(axis)
    return lax.ppermute(block, axis, [(i, (i + offset) % size) for i in range(size)])


def swap(block, axis, bits=1):
    size = lax.axis_size(axis)
    return lax.ppermute(block, axis, [(i, i ^ bits) for i in range(size)])


def exchange(block, axis):
    size = lax.axis_size(axis)
    if size & (size - 1):
        return [shift(block, axis, k) for k in range(1, size)]
    return [swap(block, axis, k) for k in range(size - 1, 0, -1)]


def on_device(queries, past_cache, lengths, live_counts, adapter_index, adapter_down, adapter_up):
    slots, cols = queries.shape
    heads = cols // HEAD_DIM
    replicas = lax.axis_size("replica")
    holders = 2 if replicas % 2 == 0 else 1
    sources = replicas // holders
    pad = 16
    while pad < slots:
        pad *= 2
    downs = [adapter_down] + [swap(adapter_down, "replica") for _ in range(1, holders)]
    rows = attend(queries, past_cache, lengths, adapter_index)
    gathered = [shift(rows, "replica", holders * k) for k in range(1, sources)]
    attention, alive = attention_out(live_counts, rows, slots, heads)
    own = lower_own(adapter_down, rows, slots, heads, pad)
    later_up = lax.optimization_barrier((adapter_up, alive, own[0]))[0]
    ups = [adapter_up] + [swap(later_up, "replica") for _ in range(1, holders)]
    partial, index = lower(own, downs, gathered, slots, heads, pad)
    partials = [partial] + exchange(partial, "tensor")
    widened = raise_rows(index, ups, partials, slots, heads, sources - 1)
    returned = [shift(widened[k - 1], "replica", -holders * k) for k in range(1, sources)]
    own = raise_own(index, ups, partials, slots)
    adapted = adapted_out(alive, own, returned, slots, heads)
    return (attention, adapted)


def solution(mesh):
    in_specs = (
        P(("groups", "replica"), "tensor"),
        P(None, ("groups", "replica"), None, "tensor"),
        P(("groups", "replica")),
        P(("groups", "replica")),
        P(("groups", "replica")),
        P("replica", None, "tensor"),
        P("replica", None, "tensor"),
    )
    out_specs = (P(("groups", "replica"), "tensor"), P(("groups", "replica"), "tensor"))
    return jax.shard_map(
        on_device, mesh=mesh, in_specs=in_specs, out_specs=out_specs, check_vma=False
    )
```

```python
import functools
import math

import jax
import jax.numpy as jnp
from jax import lax
from jax.experimental import pallas as pl
from jax.experimental.pallas import tpu as pltpu
from jax.sharding import PartitionSpec as P

HEAD_DIM = 128
STAY = 16
SCALING = 2.0
LANES = 128
GROUP = 16
DIGIT = 7

VMEM = pl.BlockSpec(memory_space=pltpu.VMEM)
SMEM = pl.BlockSpec(memory_space=pltpu.SMEM)
HBM = pl.BlockSpec(memory_space=pltpu.HBM)
PARAMS = pltpu.CompilerParams(vmem_limit_bytes=16 * 2**20)


class Lines:
    def __init__(self, slots, heads):
        self.slots, self.heads, self.cols = slots, heads, heads * HEAD_DIM
        self.groups, self.left = divmod(slots, GROUP)
        self.main = self.groups * GROUP
        self.tiles = -(-self.left * heads // GROUP)
        self.start = self.groups * self.cols
        self.width = self.start + self.tiles * HEAD_DIM
        self.small = (max(1, self.tiles) * GROUP, HEAD_DIM)

    def tile(self, number):
        return slice(self.start + number * HEAD_DIM, self.start + (number + 1) * HEAD_DIM)

    def load_left(self, refs, small):
        for number in range(self.tiles):
            total = refs[0][:, self.tile(number)].astype(jnp.float32)
            for ref in refs[1:]:
                total += ref[:, self.tile(number)].astype(jnp.float32)
            small[number * GROUP : (number + 1) * GROUP, :] = total

    def left_rows(self, head, small):
        return small[pl.ds(head, self.left, stride=self.heads), :]

    def column(self, refs, head, small):
        pieces = []
        for group in range(self.groups):
            lanes = slice(group * self.cols + head * HEAD_DIM, group * self.cols + (head + 1) * HEAD_DIM)
            total = refs[0][:, lanes].astype(jnp.float32)
            for ref in refs[1:]:
                total += ref[:, lanes].astype(jnp.float32)
            pieces.append(total)
        if self.left:
            pieces.append(self.left_rows(head, small))
        return jnp.concatenate(pieces, axis=0)


def attend_kernel(
    q_ref, cache_ref, lengths_ref, index_ref, rows_ref,
    q_flat, lengths, index, keys, values, q_rows, o_rows, small, large,
):
    slots, cols = q_ref.shape
    heads = cols // HEAD_DIM
    context, width = keys.shape[1:]
    key_heads = width // HEAD_DIM
    group = heads // key_heads
    fetches = []
    for number, (source, target) in enumerate(((q_ref, q_flat), (lengths_ref, lengths), (index_ref, index))):
        fetches.append(pltpu.make_async_copy(source, target, small.at[number]))
        fetches[-1].start()
    copies = []
    for side, buffer in enumerate((keys, values)):
        copies.append(pltpu.make_async_copy(cache_ref.at[side], buffer, large.at[side]))
        copies[-1].start()
    for fetch in fetches:
        fetch.wait()
    for head in range(heads):
        block = q_flat[:, head * HEAD_DIM : (head + 1) * HEAD_DIM]
        q_rows[pl.ds(head, slots, stride=heads), :] = block.astype(jnp.float32)
    owner = lax.broadcasted_iota(jnp.int32, (heads, HEAD_DIM), 0) // group
    position = lax.broadcasted_iota(jnp.int32, (heads, context), 1)
    weights = []
    copies[0].wait()
    for slot in range(slots):
        rows = q_rows[slot * heads : (slot + 1) * heads, :]
        wide = [jnp.where(owner == k, rows, 0.0) for k in range(key_heads)]
        wide = jnp.concatenate(wide, axis=1).astype(jnp.bfloat16)
        scores = lax.dot_general(
            wide, keys[slot], (((1,), (1,)), ((), ())), preferred_element_type=jnp.float32
        ) / math.sqrt(HEAD_DIM)
        scores = jnp.where(position < lengths[slot], scores, -jnp.inf)
        raised = jnp.exp(scores - jnp.max(scores, axis=-1, keepdims=True))
        weights.append((raised / jnp.sum(raised, axis=-1, keepdims=True)).astype(jnp.bfloat16))
    copies[1].wait()
    for slot in range(slots):
        mixed = jnp.dot(weights[slot], values[slot], preferred_element_type=jnp.float32)
        rows = mixed[:, :HEAD_DIM]
        for k in range(1, key_heads):
            rows = jnp.where(owner == k, mixed[:, k * HEAD_DIM : (k + 1) * HEAD_DIM], rows)
        o_rows[slot * heads : (slot + 1) * heads, :] = rows
    lines = Lines(slots, heads)
    for group in range(lines.groups):
        for head in range(heads):
            lanes = slice(group * cols + head * HEAD_DIM, group * cols + (head + 1) * HEAD_DIM)
            block = o_rows[pl.ds(group * GROUP * heads + head, GROUP, stride=heads), :]
            rows_ref[:, lanes] = block.astype(jnp.bfloat16)
    if lines.tiles * GROUP > lines.left * heads:
        o_rows[slots * heads :, :] = jnp.zeros((lines.tiles * GROUP - lines.left * heads, HEAD_DIM), jnp.float32)
    for number in range(lines.tiles):
        first = lines.main * heads + number * GROUP
        rows_ref[:, lines.tile(number)] = o_rows[first : first + GROUP, :].astype(jnp.bfloat16)
    lane = lax.broadcasted_iota(jnp.int32, (16, LANES), 1)
    line = lax.broadcasted_iota(jnp.int32, (16, LANES), 0)
    named = jnp.zeros((16, LANES), jnp.int32)
    for slot in range(slots):
        named = jnp.where(lane == slot, index[slot], named)
    digits = jnp.where(line == 0, named >> DIGIT, named & ((1 << DIGIT) - 1))
    rows_ref[:, lines.width :] = digits.astype(jnp.float32).astype(jnp.bfloat16)


def attend(queries, past_cache, lengths, adapter_index):
    slots, cols = queries.shape
    heads = cols // HEAD_DIM
    lines = Lines(slots, heads)
    buffer = pltpu.VMEM(past_cache.shape[1:], past_cache.dtype)
    return pl.pallas_call(
        attend_kernel,
        out_shape=jax.ShapeDtypeStruct((GROUP, lines.width + LANES), jnp.bfloat16),
        in_specs=[HBM] * 4,
        out_specs=VMEM,
        scratch_shapes=[
            pltpu.VMEM(queries.shape, queries.dtype),
            pltpu.SMEM(lengths.shape, jnp.int32),
            pltpu.SMEM(adapter_index.shape, jnp.int32),
            buffer,
            buffer,
            pltpu.VMEM((slots * heads, HEAD_DIM), jnp.float32),
            pltpu.VMEM((lines.main * heads + lines.tiles * GROUP, HEAD_DIM), jnp.float32),
            pltpu.SemaphoreType.DMA((3,)),
            pltpu.SemaphoreType.DMA((2,)),
        ],
        cost_estimate=pl.CostEstimate(
            flops=4 * past_cache.size * heads, bytes_accessed=2 * past_cache.size, transcendentals=0
        ),
        compiler_params=PARAMS,
        name="attend",
    )(*[pltpu.with_memory_space_constraint(x, pltpu.HBM) for x in (queries, past_cache, lengths, adapter_index)])


def alive_lines(live_ref, slots):
    slot = lax.broadcasted_iota(jnp.int32, (slots, HEAD_DIM), 0)
    return (slot >= STAY) | (slot < live_ref[0])


def attention_kernel(slots, heads, live_ref, rows_ref, out_ref, alive_ref, small):
    lines = Lines(slots, heads)
    alive = alive_lines(live_ref, slots)
    alive_ref[...] = alive.astype(jnp.float32)
    lines.load_left([rows_ref], small)
    for head in range(heads):
        block = jnp.where(alive, lines.column([rows_ref], head, small), 0.0)
        out_ref[:, head * HEAD_DIM : (head + 1) * HEAD_DIM] = block.astype(out_ref.dtype)


def attention_out(live, rows, slots, heads):
    return pl.pallas_call(
        functools.partial(attention_kernel, slots, heads),
        out_shape=(
            jax.ShapeDtypeStruct((slots, heads * HEAD_DIM), jnp.bfloat16),
            jax.ShapeDtypeStruct((slots, HEAD_DIM), jnp.float32),
        ),
        in_specs=[SMEM, VMEM],
        out_specs=(VMEM, VMEM),
        scratch_shapes=[pltpu.VMEM(Lines(slots, heads).small, jnp.float32)],
        compiler_params=PARAMS,
        name="attention_out",
    )(live, rows)


def adapted_kernel(slots, heads, alive_ref, own_ref, *refs):
    rows_refs, out_ref, small = refs[:-2], refs[-2], refs[-1]
    lines = Lines(slots, heads)
    alive = alive_ref[...] > 0
    if rows_refs:
        lines.load_left(rows_refs, small)
    for head in range(heads):
        block = own_ref[:, head * HEAD_DIM : (head + 1) * HEAD_DIM]
        if rows_refs:
            block += lines.column(rows_refs, head, small)
        out_ref[:, head * HEAD_DIM : (head + 1) * HEAD_DIM] = jnp.where(alive, block, 0.0).astype(out_ref.dtype)


def adapted_out(alive, own, rows, slots, heads):
    return pl.pallas_call(
        functools.partial(adapted_kernel, slots, heads),
        out_shape=jax.ShapeDtypeStruct((slots, heads * HEAD_DIM), jnp.bfloat16),
        in_specs=[VMEM] * (2 + len(rows)),
        out_specs=VMEM,
        scratch_shapes=[pltpu.VMEM(Lines(slots, heads).small, jnp.float32)],
        compiler_params=PARAMS,
        name="adapted_out",
    )(alive, own, *rows)


def first_adapter(holder, local_count):
    return (lax.axis_index("replica") ^ holder) * local_count


def unfold_rows(rows_ref, slots, heads, pad, small, wide_ref, first):
    lines = Lines(slots, heads)
    for group in range(lines.groups):
        at = first + group * GROUP
        wide_ref[at : at + GROUP, :] = rows_ref[:, group * lines.cols : (group + 1) * lines.cols]
    lines.load_left([rows_ref], small)
    if pad > lines.main:
        for head in range(heads):
            block = jnp.zeros((pad - slots, HEAD_DIM), jnp.float32)
            if lines.left:
                block = jnp.concatenate([lines.left_rows(head, small), block], axis=0)
            lanes = slice(head * HEAD_DIM, (head + 1) * HEAD_DIM)
            wide_ref[first + lines.main : first + pad, lanes] = block.astype(jnp.bfloat16)
    digits = rows_ref[:, lines.width :].astype(jnp.float32).astype(jnp.int32)
    return ((digits[0:1, :] << DIGIT) + digits[1:2, :])[:, :pad]


def own_lines_kernel(slots, heads, pad, rows_ref, index_ref, wide_ref, small):
    index_ref[...] = unfold_rows(rows_ref, slots, heads, pad, small, wide_ref, 0)


def own_lines(rows, slots, heads, pad):
    return pl.pallas_call(
        functools.partial(own_lines_kernel, slots, heads, pad),
        out_shape=(
            jax.ShapeDtypeStruct((1, pad), jnp.int32),
            jax.ShapeDtypeStruct((pad, heads * HEAD_DIM), jnp.bfloat16),
        ),
        in_specs=[VMEM],
        out_specs=[VMEM] * 2,
        scratch_shapes=[pltpu.VMEM(Lines(slots, heads).small, jnp.float32)],
        compiler_params=PARAMS,
        name="own_lines",
    )(rows)


def lower_kernel(slots, heads, pad, sources, holders, own_index_ref, own_wide_ref, *refs):
    down_refs, rows_refs = refs[:holders], refs[holders : holders + sources]
    partial_ref, index_ref, small, wide = refs[-4:]
    local_count, rank, cols = down_refs[0].shape
    named = []
    for source in range(sources):
        named.append(unfold_rows(rows_refs[source], slots, heads, pad, small, wide, source * pad))
    named.append(own_index_ref[...])
    for block in range(sources + 1):
        index_ref[block : block + 1, :] = named[block - 1]
    down = jnp.concatenate([ref[...].reshape(local_count * rank, cols) for ref in down_refs], axis=0)
    rows = own_wide_ref[...]
    if sources:
        rows = jnp.concatenate([wide[...], rows], axis=0)
    every = lax.dot_general(down, rows, (((1,), (1,)), ((), ())), preferred_element_type=jnp.float32)
    named = jnp.concatenate(named, axis=1)
    total = jnp.zeros((rank, named.shape[1]), jnp.float32)
    for holder in range(holders):
        for local in range(local_count):
            line = (holder * local_count + local) * rank
            mine = named == first_adapter(holder, local_count) + local
            total += jnp.where(mine, every[line : line + rank, :], 0.0)
    partial_ref[...] = total


def lower(own, downs, rows, slots, heads, pad):
    sources = len(rows)
    rank = downs[0].shape[1]
    return pl.pallas_call(
        functools.partial(lower_kernel, slots, heads, pad, sources, len(downs)),
        out_shape=(
            jax.ShapeDtypeStruct((rank, (1 + sources) * pad), jnp.float32),
            jax.ShapeDtypeStruct((1 + sources, pad), jnp.int32),
        ),
        in_specs=[VMEM] * (2 + len(downs) + sources),
        out_specs=[VMEM] * 2,
        scratch_shapes=[
            pltpu.VMEM(Lines(slots, heads).small, jnp.float32),
            pltpu.VMEM((max(1, sources) * pad, heads * HEAD_DIM), jnp.bfloat16),
        ],
        cost_estimate=pl.CostEstimate(flops=2 * 10**10, bytes_accessed=0, transcendentals=0),
        compiler_params=PARAMS,
        name="lower",
    )(*own, *downs, *rows)


def spread_ranks(index, total, holders, local_count):
    total = SCALING * total
    spread = []
    for holder in range(holders):
        for local in range(local_count):
            mine = index == first_adapter(holder, local_count) + local
            spread.append(jnp.where(mine, total, 0.0))
    return jnp.concatenate(spread, axis=0).astype(jnp.bfloat16)


def stack_ups(up_refs):
    local_count, rank, cols = up_refs[0].shape
    up = [up_ref[...].reshape(local_count * rank, cols) for up_ref in up_refs]
    return jnp.concatenate(up, axis=0)


def raise_kernel(slots, heads, sources, holders, index_ref, *refs):
    up_refs, partials, outs, small = refs[:holders], refs[holders : -sources - 1], refs[-sources - 1 : -1], refs[-1]
    local_count, rank, cols = up_refs[0].shape
    lines = Lines(slots, heads)
    up = stack_ups(up_refs)
    packed = partials[0][...]
    for other in partials[1:]:
        packed += other[...]
    pad = index_ref.shape[1]
    for source in range(sources):
        total = packed[:, source * pad : (source + 1) * pad]
        spread = spread_ranks(index_ref[1 + source : 2 + source, :], total, holders, local_count)
        wide = lax.dot_general(spread, up, (((0,), (0,)), ((), ())), preferred_element_type=jnp.float32)
        out_ref = outs[source]
        for group in range(lines.groups):
            block = wide[group * GROUP : (group + 1) * GROUP, :]
            out_ref[:, group * cols : (group + 1) * cols] = block.astype(jnp.bfloat16)
        if lines.left:
            small[...] = jnp.zeros(small.shape, jnp.float32)
            for head in range(heads):
                block = wide[lines.main : slots, head * HEAD_DIM : (head + 1) * HEAD_DIM]
                small[pl.ds(head, lines.left, stride=heads), :] = block
        for number in range(lines.tiles):
            block = small[number * GROUP : (number + 1) * GROUP, :]
            out_ref[:, lines.tile(number)] = block.astype(jnp.bfloat16)


def raise_rows(index, ups, partials, slots, heads, sources):
    lines = Lines(slots, heads)
    return pl.pallas_call(
        functools.partial(raise_kernel, slots, heads, sources, len(ups)),
        out_shape=[jax.ShapeDtypeStruct((GROUP, lines.width), jnp.bfloat16)] * sources,
        in_specs=[VMEM] * (1 + len(ups) + len(partials)),
        out_specs=[VMEM] * sources,
        scratch_shapes=[pltpu.VMEM(lines.small, jnp.float32)],
        compiler_params=PARAMS,
        name="raise_rows",
    )(index, *ups, *partials)


def raise_own_kernel(slots, holders, index_ref, *refs):
    up_refs, partials, out_ref = refs[:holders], refs[holders:-1], refs[-1]
    local_count, rank, cols = up_refs[0].shape
    packed = partials[0][...]
    for other in partials[1:]:
        packed += other[...]
    total = packed[:, packed.shape[1] - index_ref.shape[1] :]
    spread = spread_ranks(index_ref[0:1, :], total, holders, local_count)
    wide = lax.dot_general(spread, stack_ups(up_refs), (((0,), (0,)), ((), ())), preferred_element_type=jnp.float32)
    out_ref[...] = wide[:slots, :]


def raise_own(index, ups, partials, slots):
    return pl.pallas_call(
        functools.partial(raise_own_kernel, slots, len(ups)),
        out_shape=jax.ShapeDtypeStruct((slots, ups[0].shape[2]), jnp.float32),
        in_specs=[VMEM] * (1 + len(ups) + len(partials)),
        out_specs=VMEM,
        compiler_params=PARAMS,
        name="raise_own",
    )(index, *ups, *partials)


def shift(block, axis, offset):
    size = lax.axis_size(axis)
    return lax.ppermute(block, axis, [(i, (i + offset) % size) for i in range(size)])


def swap(block, axis, bits=1):
    size = lax.axis_size(axis)
    return lax.ppermute(block, axis, [(i, i ^ bits) for i in range(size)])


def exchange(block, axis):
    size = lax.axis_size(axis)
    if size & (size - 1):
        return [shift(block, axis, k) for k in range(1, size)]
    return [swap(block, axis, k) for k in [*range(2, size), 1]]


def on_device(queries, past_cache, lengths, live_counts, adapter_index, adapter_down, adapter_up):
    slots, cols = queries.shape
    heads = cols // HEAD_DIM
    replicas = lax.axis_size("replica")
    holders = 2 if replicas % 2 == 0 else 1
    sources = replicas // holders
    pad = 16
    while pad < slots:
        pad *= 2
    downs = [adapter_down] + [swap(adapter_down, "replica") for _ in range(1, holders)]
    rows = attend(queries, past_cache, lengths, adapter_index)
    gathered = [shift(rows, "replica", holders * k) for k in range(1, sources)]
    attention, alive = attention_out(live_counts, rows, slots, heads)
    own = own_lines(rows, slots, heads, pad)
    later_up = lax.optimization_barrier((adapter_up, alive))[0]
    ups = [adapter_up] + [swap(later_up, "replica") for _ in range(1, holders)]
    partial, index = lower(own, downs, gathered, slots, heads, pad)
    partials = [partial] + exchange(partial, "tensor")
    widened = raise_rows(index, ups, partials, slots, heads, sources - 1)
    returned = [shift(widened[k - 1], "replica", -holders * k) for k in range(1, sources)]
    own = raise_own(index, ups, partials, slots)
    adapted = adapted_out(alive, own, returned, slots, heads)
    return (attention, adapted)


def solution(mesh):
    in_specs = (
        P(("groups", "replica"), "tensor"),
        P(None, ("groups", "replica"), None, "tensor"),
        P(("groups", "replica")),
        P(("groups", "replica")),
        P(("groups", "replica")),
        P("replica", None, "tensor"),
        P("replica", None, "tensor"),
    )
    out_specs = (P(("groups", "replica"), "tensor"), P(("groups", "replica"), "tensor"))
    return jax.shard_map(
        on_device, mesh=mesh, in_specs=in_specs, out_specs=out_specs, check_vma=False
    )
```

```python
import functools
import math

import jax
import jax.numpy as jnp
from jax import lax
from jax.experimental import pallas as pl
from jax.experimental.pallas import tpu as pltpu
from jax.sharding import PartitionSpec as P

HEAD_DIM = 128
STAY = 16
SCALING = 2.0
LANES = 128
GROUP = 16
DIGIT = 7

VMEM = pl.BlockSpec(memory_space=pltpu.VMEM)
SMEM = pl.BlockSpec(memory_space=pltpu.SMEM)
HBM = pl.BlockSpec(memory_space=pltpu.HBM)
PARAMS = pltpu.CompilerParams(vmem_limit_bytes=16 * 2**20)


class Lines:
    def __init__(self, slots, heads):
        self.slots, self.heads, self.cols = slots, heads, heads * HEAD_DIM
        self.groups, self.left = divmod(slots, GROUP)
        self.main = self.groups * GROUP
        self.tiles = -(-self.left * heads // GROUP)
        self.start = self.groups * self.cols
        self.width = self.start + self.tiles * HEAD_DIM
        self.small = (max(1, self.tiles) * GROUP, HEAD_DIM)

    def tile(self, number):
        return slice(self.start + number * HEAD_DIM, self.start + (number + 1) * HEAD_DIM)

    def load_left(self, refs, small):
        for number in range(self.tiles):
            total = refs[0][:, self.tile(number)].astype(jnp.float32)
            for ref in refs[1:]:
                total += ref[:, self.tile(number)].astype(jnp.float32)
            small[number * GROUP : (number + 1) * GROUP, :] = total

    def left_rows(self, head, small):
        return small[pl.ds(head, self.left, stride=self.heads), :]

    def column(self, refs, head, small):
        pieces = []
        for group in range(self.groups):
            lanes = slice(group * self.cols + head * HEAD_DIM, group * self.cols + (head + 1) * HEAD_DIM)
            total = refs[0][:, lanes].astype(jnp.float32)
            for ref in refs[1:]:
                total += ref[:, lanes].astype(jnp.float32)
            pieces.append(total)
        if self.left:
            pieces.append(self.left_rows(head, small))
        return jnp.concatenate(pieces, axis=0)


def attend_kernel(
    q_ref, cache_ref, lengths_ref, index_ref, rows_ref,
    q_flat, lengths, index, keys, values, q_rows, o_rows, small, large,
):
    slots, cols = q_ref.shape
    heads = cols // HEAD_DIM
    context, width = keys.shape[1:]
    key_heads = width // HEAD_DIM
    group = heads // key_heads
    fetches = []
    for number, (source, target) in enumerate(((q_ref, q_flat), (lengths_ref, lengths), (index_ref, index))):
        fetches.append(pltpu.make_async_copy(source, target, small.at[number]))
        fetches[-1].start()
    copies = []
    for side, buffer in enumerate((keys, values)):
        copies.append(pltpu.make_async_copy(cache_ref.at[side], buffer, large.at[side]))
        copies[-1].start()
    for fetch in fetches:
        fetch.wait()
    for head in range(heads):
        block = q_flat[:, head * HEAD_DIM : (head + 1) * HEAD_DIM]
        q_rows[pl.ds(head, slots, stride=heads), :] = block.astype(jnp.float32)
    owner = lax.broadcasted_iota(jnp.int32, (heads, HEAD_DIM), 0) // group
    position = lax.broadcasted_iota(jnp.int32, (heads, context), 1)
    weights = []
    copies[0].wait()
    for slot in range(slots):
        rows = q_rows[slot * heads : (slot + 1) * heads, :]
        wide = [jnp.where(owner == k, rows, 0.0) for k in range(key_heads)]
        wide = jnp.concatenate(wide, axis=1).astype(jnp.bfloat16)
        scores = lax.dot_general(
            wide, keys[slot], (((1,), (1,)), ((), ())), preferred_element_type=jnp.float32
        ) / math.sqrt(HEAD_DIM)
        scores = jnp.where(position < lengths[slot], scores, -jnp.inf)
        raised = jnp.exp(scores - jnp.max(scores, axis=-1, keepdims=True))
        weights.append((raised / jnp.sum(raised, axis=-1, keepdims=True)).astype(jnp.bfloat16))
    copies[1].wait()
    for slot in range(slots):
        mixed = jnp.dot(weights[slot], values[slot], preferred_element_type=jnp.float32)
        rows = mixed[:, :HEAD_DIM]
        for k in range(1, key_heads):
            rows = jnp.where(owner == k, mixed[:, k * HEAD_DIM : (k + 1) * HEAD_DIM], rows)
        o_rows[slot * heads : (slot + 1) * heads, :] = rows
    lines = Lines(slots, heads)
    for group in range(lines.groups):
        for head in range(heads):
            lanes = slice(group * cols + head * HEAD_DIM, group * cols + (head + 1) * HEAD_DIM)
            block = o_rows[pl.ds(group * GROUP * heads + head, GROUP, stride=heads), :]
            rows_ref[:, lanes] = block.astype(jnp.bfloat16)
    if lines.tiles * GROUP > lines.left * heads:
        o_rows[slots * heads :, :] = jnp.zeros((lines.tiles * GROUP - lines.left * heads, HEAD_DIM), jnp.float32)
    for number in range(lines.tiles):
        first = lines.main * heads + number * GROUP
        rows_ref[:, lines.tile(number)] = o_rows[first : first + GROUP, :].astype(jnp.bfloat16)
    lane = lax.broadcasted_iota(jnp.int32, (16, LANES), 1)
    line = lax.broadcasted_iota(jnp.int32, (16, LANES), 0)
    named = jnp.zeros((16, LANES), jnp.int32)
    for slot in range(slots):
        named = jnp.where(lane == slot, index[slot], named)
    digits = jnp.where(line == 0, named >> DIGIT, named & ((1 << DIGIT) - 1))
    rows_ref[:, lines.width :] = digits.astype(jnp.float32).astype(jnp.bfloat16)


def attend(queries, past_cache, lengths, adapter_index):
    slots, cols = queries.shape
    heads = cols // HEAD_DIM
    lines = Lines(slots, heads)
    buffer = pltpu.VMEM(past_cache.shape[1:], past_cache.dtype)
    return pl.pallas_call(
        attend_kernel,
        out_shape=jax.ShapeDtypeStruct((GROUP, lines.width + LANES), jnp.bfloat16),
        in_specs=[HBM] * 4,
        out_specs=VMEM,
        scratch_shapes=[
            pltpu.VMEM(queries.shape, queries.dtype),
            pltpu.SMEM(lengths.shape, jnp.int32),
            pltpu.SMEM(adapter_index.shape, jnp.int32),
            buffer,
            buffer,
            pltpu.VMEM((slots * heads, HEAD_DIM), jnp.float32),
            pltpu.VMEM((lines.main * heads + lines.tiles * GROUP, HEAD_DIM), jnp.float32),
            pltpu.SemaphoreType.DMA((3,)),
            pltpu.SemaphoreType.DMA((2,)),
        ],
        cost_estimate=pl.CostEstimate(
            flops=4 * past_cache.size * heads, bytes_accessed=2 * past_cache.size, transcendentals=0
        ),
        compiler_params=PARAMS,
        name="attend",
    )(*[pltpu.with_memory_space_constraint(x, pltpu.HBM) for x in (queries, past_cache, lengths, adapter_index)])


def alive_lines(live_ref, slots):
    slot = lax.broadcasted_iota(jnp.int32, (slots, HEAD_DIM), 0)
    return (slot >= STAY) | (slot < live_ref[0])


def attention_kernel(slots, heads, live_ref, rows_ref, out_ref, alive_ref, small):
    lines = Lines(slots, heads)
    alive = alive_lines(live_ref, slots)
    alive_ref[...] = alive.astype(jnp.float32)
    lines.load_left([rows_ref], small)
    for head in range(heads):
        block = jnp.where(alive, lines.column([rows_ref], head, small), 0.0)
        out_ref[:, head * HEAD_DIM : (head + 1) * HEAD_DIM] = block.astype(out_ref.dtype)


def attention_out(live, rows, slots, heads):
    return pl.pallas_call(
        functools.partial(attention_kernel, slots, heads),
        out_shape=(
            jax.ShapeDtypeStruct((slots, heads * HEAD_DIM), jnp.bfloat16),
            jax.ShapeDtypeStruct((slots, HEAD_DIM), jnp.float32),
        ),
        in_specs=[SMEM, VMEM],
        out_specs=(VMEM, VMEM),
        scratch_shapes=[pltpu.VMEM(Lines(slots, heads).small, jnp.float32)],
        compiler_params=PARAMS,
        name="attention_out",
    )(live, rows)


def adapted_kernel(slots, heads, alive_ref, own_ref, *refs):
    rows_refs, out_ref, small = refs[:-2], refs[-2], refs[-1]
    lines = Lines(slots, heads)
    alive = alive_ref[...] > 0
    if rows_refs:
        lines.load_left(rows_refs, small)
    for head in range(heads):
        block = own_ref[:, head * HEAD_DIM : (head + 1) * HEAD_DIM]
        if rows_refs:
            block += lines.column(rows_refs, head, small)
        out_ref[:, head * HEAD_DIM : (head + 1) * HEAD_DIM] = jnp.where(alive, block, 0.0).astype(out_ref.dtype)


def adapted_out(alive, own, rows, slots, heads):
    return pl.pallas_call(
        functools.partial(adapted_kernel, slots, heads),
        out_shape=jax.ShapeDtypeStruct((slots, heads * HEAD_DIM), jnp.bfloat16),
        in_specs=[VMEM] * (2 + len(rows)),
        out_specs=VMEM,
        scratch_shapes=[pltpu.VMEM(Lines(slots, heads).small, jnp.float32)],
        compiler_params=PARAMS,
        name="adapted_out",
    )(alive, own, *rows)


def first_adapter(holder, local_count):
    return (lax.axis_index("replica") ^ holder) * local_count


def unfold_rows(rows_ref, slots, heads, pad, small, wide_ref, first):
    lines = Lines(slots, heads)
    for group in range(lines.groups):
        at = first + group * GROUP
        wide_ref[at : at + GROUP, :] = rows_ref[:, group * lines.cols : (group + 1) * lines.cols]
    lines.load_left([rows_ref], small)
    if pad > lines.main:
        for head in range(heads):
            block = jnp.zeros((pad - slots, HEAD_DIM), jnp.float32)
            if lines.left:
                block = jnp.concatenate([lines.left_rows(head, small), block], axis=0)
            lanes = slice(head * HEAD_DIM, (head + 1) * HEAD_DIM)
            wide_ref[first + lines.main : first + pad, lanes] = block.astype(jnp.bfloat16)
    digits = rows_ref[:, lines.width :].astype(jnp.float32).astype(jnp.int32)
    return ((digits[0:1, :] << DIGIT) + digits[1:2, :])[:, :pad]


def own_lines_kernel(slots, heads, pad, rows_ref, index_ref, wide_ref, small):
    index_ref[...] = unfold_rows(rows_ref, slots, heads, pad, small, wide_ref, 0)


def own_lines(rows, slots, heads, pad):
    return pl.pallas_call(
        functools.partial(own_lines_kernel, slots, heads, pad),
        out_shape=(
            jax.ShapeDtypeStruct((1, pad), jnp.int32),
            jax.ShapeDtypeStruct((pad, heads * HEAD_DIM), jnp.bfloat16),
        ),
        in_specs=[VMEM],
        out_specs=[VMEM] * 2,
        scratch_shapes=[pltpu.VMEM(Lines(slots, heads).small, jnp.float32)],
        compiler_params=PARAMS,
        name="own_lines",
    )(rows)


def lower_kernel(slots, heads, pad, sources, holders, own_index_ref, own_wide_ref, *refs):
    down_refs, rows_refs = refs[:holders], refs[holders : holders + sources]
    partial_ref, index_ref, small, wide = refs[-4:]
    local_count, rank, cols = down_refs[0].shape
    named = []
    for source in range(sources):
        named.append(unfold_rows(rows_refs[source], slots, heads, pad, small, wide, source * pad))
    named.append(own_index_ref[...])
    for block in range(sources + 1):
        index_ref[block : block + 1, :] = named[block - 1]
    down = jnp.concatenate([ref[...].reshape(local_count * rank, cols) for ref in down_refs], axis=0)
    lines = Lines(slots, heads)
    blocks = []
    for source in range(sources):
        for group in range(lines.groups):
            blocks.append(rows_refs[source][:, group * cols : (group + 1) * cols])
        if pad > lines.main:
            blocks.append(wide[source * pad + lines.main : (source + 1) * pad, :])
    rows = jnp.concatenate(blocks + [own_wide_ref[...]], axis=0)
    every = lax.dot_general(down, rows, (((1,), (1,)), ((), ())), preferred_element_type=jnp.float32)
    named = jnp.concatenate(named, axis=1)
    total = jnp.zeros((rank, named.shape[1]), jnp.float32)
    for holder in range(holders):
        for local in range(local_count):
            line = (holder * local_count + local) * rank
            mine = named == first_adapter(holder, local_count) + local
            total += jnp.where(mine, every[line : line + rank, :], 0.0)
    partial_ref[...] = total


def lower(own, downs, rows, slots, heads, pad):
    sources = len(rows)
    rank = downs[0].shape[1]
    return pl.pallas_call(
        functools.partial(lower_kernel, slots, heads, pad, sources, len(downs)),
        out_shape=(
            jax.ShapeDtypeStruct((rank, (1 + sources) * pad), jnp.float32),
            jax.ShapeDtypeStruct((1 + sources, pad), jnp.int32),
        ),
        in_specs=[VMEM] * (2 + len(downs) + sources),
        out_specs=[VMEM] * 2,
        scratch_shapes=[
            pltpu.VMEM(Lines(slots, heads).small, jnp.float32),
            pltpu.VMEM((max(1, sources) * pad, heads * HEAD_DIM), jnp.bfloat16),
        ],
        cost_estimate=pl.CostEstimate(flops=2 * 10**10, bytes_accessed=0, transcendentals=0),
        compiler_params=PARAMS,
        name="lower",
    )(*own, *downs, *rows)


def spread_ranks(index, total, holders, local_count):
    total = SCALING * total
    spread = []
    for holder in range(holders):
        for local in range(local_count):
            mine = index == first_adapter(holder, local_count) + local
            spread.append(jnp.where(mine, total, 0.0))
    return jnp.concatenate(spread, axis=0).astype(jnp.bfloat16)


def stack_ups(up_refs):
    local_count, rank, cols = up_refs[0].shape
    up = [up_ref[...].reshape(local_count * rank, cols) for up_ref in up_refs]
    return jnp.concatenate(up, axis=0)


def raise_kernel(slots, heads, sources, holders, index_ref, *refs):
    up_refs, partials, outs, small = refs[:holders], refs[holders : -sources - 1], refs[-sources - 1 : -1], refs[-1]
    local_count, rank, cols = up_refs[0].shape
    lines = Lines(slots, heads)
    up = stack_ups(up_refs)
    packed = partials[0][...]
    for other in partials[1:]:
        packed += other[...]
    pad = index_ref.shape[1]
    for source in range(sources):
        total = packed[:, source * pad : (source + 1) * pad]
        spread = spread_ranks(index_ref[1 + source : 2 + source, :], total, holders, local_count)
        wide = lax.dot_general(spread, up, (((0,), (0,)), ((), ())), preferred_element_type=jnp.float32)
        out_ref = outs[source]
        for group in range(lines.groups):
            block = wide[group * GROUP : (group + 1) * GROUP, :]
            out_ref[:, group * cols : (group + 1) * cols] = block.astype(jnp.bfloat16)
        if lines.left:
            small[...] = jnp.zeros(small.shape, jnp.float32)
            for head in range(heads):
                block = wide[lines.main : slots, head * HEAD_DIM : (head + 1) * HEAD_DIM]
                small[pl.ds(head, lines.left, stride=heads), :] = block
        for number in range(lines.tiles):
            block = small[number * GROUP : (number + 1) * GROUP, :]
            out_ref[:, lines.tile(number)] = block.astype(jnp.bfloat16)


def raise_rows(index, ups, partials, slots, heads, sources):
    lines = Lines(slots, heads)
    return pl.pallas_call(
        functools.partial(raise_kernel, slots, heads, sources, len(ups)),
        out_shape=[jax.ShapeDtypeStruct((GROUP, lines.width), jnp.bfloat16)] * sources,
        in_specs=[VMEM] * (1 + len(ups) + len(partials)),
        out_specs=[VMEM] * sources,
        scratch_shapes=[pltpu.VMEM(lines.small, jnp.float32)],
        compiler_params=PARAMS,
        name="raise_rows",
    )(index, *ups, *partials)


def raise_own_kernel(slots, holders, index_ref, *refs):
    up_refs, partials, out_ref = refs[:holders], refs[holders:-1], refs[-1]
    local_count, rank, cols = up_refs[0].shape
    packed = partials[0][...]
    for other in partials[1:]:
        packed += other[...]
    total = packed[:, packed.shape[1] - index_ref.shape[1] :]
    spread = spread_ranks(index_ref[0:1, :], total, holders, local_count)
    wide = lax.dot_general(spread, stack_ups(up_refs), (((0,), (0,)), ((), ())), preferred_element_type=jnp.float32)
    out_ref[...] = wide[:slots, :]


def raise_own(index, ups, partials, slots):
    return pl.pallas_call(
        functools.partial(raise_own_kernel, slots, len(ups)),
        out_shape=jax.ShapeDtypeStruct((slots, ups[0].shape[2]), jnp.float32),
        in_specs=[VMEM] * (1 + len(ups) + len(partials)),
        out_specs=VMEM,
        compiler_params=PARAMS,
        name="raise_own",
    )(index, *ups, *partials)


def shift(block, axis, offset):
    size = lax.axis_size(axis)
    return lax.ppermute(block, axis, [(i, (i + offset) % size) for i in range(size)])


def swap(block, axis, bits=1):
    size = lax.axis_size(axis)
    return lax.ppermute(block, axis, [(i, i ^ bits) for i in range(size)])


def exchange(block, axis):
    size = lax.axis_size(axis)
    if size & (size - 1):
        return [shift(block, axis, k) for k in range(1, size)]
    return [swap(block, axis, k) for k in [*range(2, size), 1]]


def on_device(queries, past_cache, lengths, live_counts, adapter_index, adapter_down, adapter_up):
    slots, cols = queries.shape
    heads = cols // HEAD_DIM
    replicas = lax.axis_size("replica")
    holders = 2 if replicas % 2 == 0 else 1
    sources = replicas // holders
    pad = 16
    while pad < slots:
        pad *= 2
    downs = [adapter_down] + [swap(adapter_down, "replica") for _ in range(1, holders)]
    rows = attend(queries, past_cache, lengths, adapter_index)
    gathered = [shift(rows, "replica", holders * k) for k in range(1, sources)]
    attention, alive = attention_out(live_counts, rows, slots, heads)
    own = own_lines(rows, slots, heads, pad)
    later_up = lax.optimization_barrier((adapter_up, alive))[0]
    ups = [adapter_up] + [swap(later_up, "replica") for _ in range(1, holders)]
    partial, index = lower(own, downs, gathered, slots, heads, pad)
    partials = [partial] + exchange(partial, "tensor")
    widened = raise_rows(index, ups, partials, slots, heads, sources - 1)
    returned = [shift(widened[k - 1], "replica", -holders * k) for k in range(1, sources)]
    own = raise_own(index, ups, partials, slots)
    adapted = adapted_out(alive, own, returned, slots, heads)
    return (attention, adapted)


def solution(mesh):
    in_specs = (
        P(("groups", "replica"), "tensor"),
        P(None, ("groups", "replica"), None, "tensor"),
        P(("groups", "replica")),
        P(("groups", "replica")),
        P(("groups", "replica")),
        P("replica", None, "tensor"),
        P("replica", None, "tensor"),
    )
    out_specs = (P(("groups", "replica"), "tensor"), P(("groups", "replica"), "tensor"))
    return jax.shard_map(
        on_device, mesh=mesh, in_specs=in_specs, out_specs=out_specs, check_vma=False
    )
```

```python
import functools
import math

import jax
import jax.numpy as jnp
from jax import lax
from jax.experimental import pallas as pl
from jax.experimental.pallas import tpu as pltpu
from jax.sharding import PartitionSpec as P

HEAD_DIM = 128
STAY = 16
SCALING = 2.0
LANES = 128
GROUP = 16
COLUMNS = 512
DIGIT = 7

VMEM = pl.BlockSpec(memory_space=pltpu.VMEM)
SMEM = pl.BlockSpec(memory_space=pltpu.SMEM)
HBM = pl.BlockSpec(memory_space=pltpu.HBM)
PARAMS = pltpu.CompilerParams(vmem_limit_bytes=16 * 2**20)


class Lines:
    def __init__(self, slots, heads):
        self.slots, self.heads, self.cols = slots, heads, heads * HEAD_DIM
        self.groups, self.left = divmod(slots, GROUP)
        self.main = self.groups * GROUP
        self.tiles = -(-self.left * heads // GROUP)
        self.start = self.groups * self.cols
        self.width = self.start + self.tiles * HEAD_DIM
        self.small = (max(1, self.tiles) * GROUP, HEAD_DIM)

    def tile(self, number):
        return slice(self.start + number * HEAD_DIM, self.start + (number + 1) * HEAD_DIM)

    def load_left(self, refs, small):
        for number in range(self.tiles):
            total = refs[0][:, self.tile(number)].astype(jnp.float32)
            for ref in refs[1:]:
                total += ref[:, self.tile(number)].astype(jnp.float32)
            small[number * GROUP : (number + 1) * GROUP, :] = total

    def left_rows(self, head, small):
        return small[pl.ds(head, self.left, stride=self.heads), :]

    def column(self, refs, head, small):
        pieces = []
        for group in range(self.groups):
            lanes = slice(group * self.cols + head * HEAD_DIM, group * self.cols + (head + 1) * HEAD_DIM)
            total = refs[0][:, lanes].astype(jnp.float32)
            for ref in refs[1:]:
                total += ref[:, lanes].astype(jnp.float32)
            pieces.append(total)
        if self.left:
            pieces.append(self.left_rows(head, small))
        return jnp.concatenate(pieces, axis=0)


def attend_kernel(
    q_ref, cache_ref, lengths_ref, index_ref, rows_ref,
    q_flat, lengths, index, keys, values, q_rows, o_rows, small, large,
):
    slots, cols = q_ref.shape
    heads = cols // HEAD_DIM
    context, width = keys.shape[1:]
    key_heads = width // HEAD_DIM
    group = heads // key_heads
    fetches = []
    for number, (source, target) in enumerate(((q_ref, q_flat), (lengths_ref, lengths), (index_ref, index))):
        fetches.append(pltpu.make_async_copy(source, target, small.at[number]))
        fetches[-1].start()
    copies = []
    for side, buffer in enumerate((keys, values)):
        copies.append(pltpu.make_async_copy(cache_ref.at[side], buffer, large.at[side]))
        copies[-1].start()
    for fetch in fetches:
        fetch.wait()
    for head in range(heads):
        block = q_flat[:, head * HEAD_DIM : (head + 1) * HEAD_DIM]
        q_rows[pl.ds(head, slots, stride=heads), :] = block.astype(jnp.float32)
    owner = lax.broadcasted_iota(jnp.int32, (heads, HEAD_DIM), 0) // group
    position = lax.broadcasted_iota(jnp.int32, (heads, context), 1)
    weights = []
    copies[0].wait()
    for slot in range(slots):
        rows = q_rows[slot * heads : (slot + 1) * heads, :]
        wide = [jnp.where(owner == k, rows, 0.0) for k in range(key_heads)]
        wide = jnp.concatenate(wide, axis=1).astype(jnp.bfloat16)
        scores = lax.dot_general(
            wide, keys[slot], (((1,), (1,)), ((), ())), preferred_element_type=jnp.float32
        ) / math.sqrt(HEAD_DIM)
        scores = jnp.where(position < lengths[slot], scores, -jnp.inf)
        raised = jnp.exp(scores - jnp.max(scores, axis=-1, keepdims=True))
        weights.append((raised / jnp.sum(raised, axis=-1, keepdims=True)).astype(jnp.bfloat16))
    copies[1].wait()
    for slot in range(slots):
        mixed = jnp.dot(weights[slot], values[slot], preferred_element_type=jnp.float32)
        rows = mixed[:, :HEAD_DIM]
        for k in range(1, key_heads):
            rows = jnp.where(owner == k, mixed[:, k * HEAD_DIM : (k + 1) * HEAD_DIM], rows)
        o_rows[slot * heads : (slot + 1) * heads, :] = rows
    lines = Lines(slots, heads)
    for group in range(lines.groups):
        for head in range(heads):
            lanes = slice(group * cols + head * HEAD_DIM, group * cols + (head + 1) * HEAD_DIM)
            block = o_rows[pl.ds(group * GROUP * heads + head, GROUP, stride=heads), :]
            rows_ref[:, lanes] = block.astype(jnp.bfloat16)
    if lines.tiles * GROUP > lines.left * heads:
        o_rows[slots * heads :, :] = jnp.zeros((lines.tiles * GROUP - lines.left * heads, HEAD_DIM), jnp.float32)
    for number in range(lines.tiles):
        first = lines.main * heads + number * GROUP
        rows_ref[:, lines.tile(number)] = o_rows[first : first + GROUP, :].astype(jnp.bfloat16)
    lane = lax.broadcasted_iota(jnp.int32, (16, LANES), 1)
    line = lax.broadcasted_iota(jnp.int32, (16, LANES), 0)
    named = jnp.zeros((16, LANES), jnp.int32)
    for slot in range(slots):
        named = jnp.where(lane == slot, index[slot], named)
    digits = jnp.where(line == 0, named >> DIGIT, named & ((1 << DIGIT) - 1))
    rows_ref[:, lines.width :] = digits.astype(jnp.float32).astype(jnp.bfloat16)


def attend(queries, past_cache, lengths, adapter_index):
    slots, cols = queries.shape
    heads = cols // HEAD_DIM
    lines = Lines(slots, heads)
    buffer = pltpu.VMEM(past_cache.shape[1:], past_cache.dtype)
    return pl.pallas_call(
        attend_kernel,
        out_shape=jax.ShapeDtypeStruct((GROUP, lines.width + LANES), jnp.bfloat16),
        in_specs=[HBM] * 4,
        out_specs=VMEM,
        scratch_shapes=[
            pltpu.VMEM(queries.shape, queries.dtype),
            pltpu.SMEM(lengths.shape, jnp.int32),
            pltpu.SMEM(adapter_index.shape, jnp.int32),
            buffer,
            buffer,
            pltpu.VMEM((slots * heads, HEAD_DIM), jnp.float32),
            pltpu.VMEM((lines.main * heads + lines.tiles * GROUP, HEAD_DIM), jnp.float32),
            pltpu.SemaphoreType.DMA((3,)),
            pltpu.SemaphoreType.DMA((2,)),
        ],
        cost_estimate=pl.CostEstimate(
            flops=4 * past_cache.size * heads, bytes_accessed=2 * past_cache.size, transcendentals=0
        ),
        compiler_params=PARAMS,
        name="attend",
    )(*[pltpu.with_memory_space_constraint(x, pltpu.HBM) for x in (queries, past_cache, lengths, adapter_index)])


def alive_lines(live_ref, slots):
    slot = lax.broadcasted_iota(jnp.int32, (slots, HEAD_DIM), 0)
    return (slot >= STAY) | (slot < live_ref[0])


def attention_kernel(slots, heads, live_ref, rows_ref, out_ref, alive_ref, small):
    lines = Lines(slots, heads)
    alive = alive_lines(live_ref, slots)
    alive_ref[...] = alive.astype(jnp.float32)
    lines.load_left([rows_ref], small)
    for head in range(heads):
        block = jnp.where(alive, lines.column([rows_ref], head, small), 0.0)
        out_ref[:, head * HEAD_DIM : (head + 1) * HEAD_DIM] = block.astype(out_ref.dtype)


def attention_out(live, rows, slots, heads):
    return pl.pallas_call(
        functools.partial(attention_kernel, slots, heads),
        out_shape=(
            jax.ShapeDtypeStruct((slots, heads * HEAD_DIM), jnp.bfloat16),
            jax.ShapeDtypeStruct((slots, HEAD_DIM), jnp.float32),
        ),
        in_specs=[SMEM, VMEM],
        out_specs=(VMEM, VMEM),
        scratch_shapes=[pltpu.VMEM(Lines(slots, heads).small, jnp.float32)],
        compiler_params=PARAMS,
        name="attention_out",
    )(live, rows)


def adapted_kernel(slots, heads, alive_ref, own_ref, *refs):
    rows_refs, out_ref, small = refs[:-2], refs[-2], refs[-1]
    lines = Lines(slots, heads)
    alive = alive_ref[...] > 0
    if rows_refs:
        lines.load_left(rows_refs, small)
    for head in range(heads):
        block = own_ref[:, head * HEAD_DIM : (head + 1) * HEAD_DIM]
        if rows_refs:
            block += lines.column(rows_refs, head, small)
        out_ref[:, head * HEAD_DIM : (head + 1) * HEAD_DIM] = jnp.where(alive, block, 0.0).astype(out_ref.dtype)


def adapted_out(alive, own, rows, slots, heads):
    return pl.pallas_call(
        functools.partial(adapted_kernel, slots, heads),
        out_shape=jax.ShapeDtypeStruct((slots, heads * HEAD_DIM), jnp.bfloat16),
        in_specs=[VMEM] * (2 + len(rows)),
        out_specs=VMEM,
        scratch_shapes=[pltpu.VMEM(Lines(slots, heads).small, jnp.float32)],
        compiler_params=PARAMS,
        name="adapted_out",
    )(alive, own, *rows)


def first_adapter(holder, local_count):
    return (lax.axis_index("replica") ^ holder) * local_count


def unfold_rows(rows_ref, slots, heads, pad, small, wide_ref, first):
    lines = Lines(slots, heads)
    for group in range(lines.groups):
        at = first + group * GROUP
        wide_ref[at : at + GROUP, :] = rows_ref[:, group * lines.cols : (group + 1) * lines.cols]
    lines.load_left([rows_ref], small)
    if pad > lines.main:
        for head in range(heads):
            block = jnp.zeros((pad - slots, HEAD_DIM), jnp.float32)
            if lines.left:
                block = jnp.concatenate([lines.left_rows(head, small), block], axis=0)
            lanes = slice(head * HEAD_DIM, (head + 1) * HEAD_DIM)
            wide_ref[first + lines.main : first + pad, lanes] = block.astype(jnp.bfloat16)
    digits = rows_ref[:, lines.width :].astype(jnp.float32).astype(jnp.int32)
    return ((digits[0:1, :] << DIGIT) + digits[1:2, :])[:, :pad]


def own_lines_kernel(slots, heads, pad, rows_ref, index_ref, wide_ref, small):
    index_ref[...] = unfold_rows(rows_ref, slots, heads, pad, small, wide_ref, 0)


def own_lines(rows, slots, heads, pad):
    return pl.pallas_call(
        functools.partial(own_lines_kernel, slots, heads, pad),
        out_shape=(
            jax.ShapeDtypeStruct((1, pad), jnp.int32),
            jax.ShapeDtypeStruct((pad, heads * HEAD_DIM), jnp.bfloat16),
        ),
        in_specs=[VMEM],
        out_specs=[VMEM] * 2,
        scratch_shapes=[pltpu.VMEM(Lines(slots, heads).small, jnp.float32)],
        compiler_params=PARAMS,
        name="own_lines",
    )(rows)


def lower_kernel(slots, heads, pad, sources, holders, own_index_ref, own_wide_ref, *refs):
    down_refs, rows_refs = refs[:holders], refs[holders : holders + sources]
    partial_ref, index_ref, small, wide = refs[-4:]
    local_count, rank, cols = down_refs[0].shape
    named = []
    for source in range(sources):
        named.append(unfold_rows(rows_refs[source], slots, heads, pad, small, wide, source * pad))
    named.append(own_index_ref[...])
    for block in range(sources + 1):
        index_ref[block : block + 1, :] = named[block - 1]
    down = jnp.concatenate([ref[...].reshape(local_count * rank, cols) for ref in down_refs], axis=0)
    rows = own_wide_ref[...]
    if sources:
        rows = jnp.concatenate([wide[...], rows], axis=0)
    every = lax.dot_general(down, rows, (((1,), (1,)), ((), ())), preferred_element_type=jnp.float32)
    named = jnp.concatenate(named, axis=1)
    total = jnp.zeros((rank, named.shape[1]), jnp.float32)
    for holder in range(holders):
        for local in range(local_count):
            line = (holder * local_count + local) * rank
            mine = named == first_adapter(holder, local_count) + local
            total += jnp.where(mine, every[line : line + rank, :], 0.0)
    partial_ref[...] = total


def lower(own, downs, rows, slots, heads, pad):
    sources = len(rows)
    rank = downs[0].shape[1]
    return pl.pallas_call(
        functools.partial(lower_kernel, slots, heads, pad, sources, len(downs)),
        out_shape=(
            jax.ShapeDtypeStruct((rank, (1 + sources) * pad), jnp.float32),
            jax.ShapeDtypeStruct((1 + sources, pad), jnp.int32),
        ),
        in_specs=[VMEM] * (2 + len(downs) + sources),
        out_specs=[VMEM] * 2,
        scratch_shapes=[
            pltpu.VMEM(Lines(slots, heads).small, jnp.float32),
            pltpu.VMEM((max(1, sources) * pad, heads * HEAD_DIM), jnp.bfloat16),
        ],
        cost_estimate=pl.CostEstimate(flops=2 * 10**10, bytes_accessed=0, transcendentals=0),
        compiler_params=PARAMS,
        name="lower",
    )(*own, *downs, *rows)


def spread_ranks(index, total, holders, local_count):
    total = SCALING * total
    spread = []
    for holder in range(holders):
        for local in range(local_count):
            mine = index == first_adapter(holder, local_count) + local
            spread.append(jnp.where(mine, total, 0.0))
    return jnp.concatenate(spread, axis=0).astype(jnp.bfloat16)


def stack_ups(up_refs):
    local_count, rank, cols = up_refs[0].shape
    up = [up_ref[...].reshape(local_count * rank, cols) for up_ref in up_refs]
    return jnp.concatenate(up, axis=0)


def raise_kernel(slots, heads, sources, holders, index_ref, *refs):
    up_refs, partials, outs, small = refs[:holders], refs[holders : -sources - 1], refs[-sources - 1 : -1], refs[-1]
    local_count, rank, cols = up_refs[0].shape
    lines = Lines(slots, heads)
    up = stack_ups(up_refs)
    packed = partials[0][...]
    for other in partials[1:]:
        packed += other[...]
    pad = index_ref.shape[1]
    for source in range(sources):
        total = packed[:, source * pad : (source + 1) * pad]
        spread = spread_ranks(index_ref[1 + source : 2 + source, :], total, holders, local_count)
        out_ref = outs[source]
        if lines.left:
            small[...] = jnp.zeros(small.shape, jnp.float32)
        step = min(cols, COLUMNS)
        for first in range(0, cols, step):
            block_up = up[:, first : first + step]
            wide = lax.dot_general(spread, block_up, (((0,), (0,)), ((), ())), preferred_element_type=jnp.float32)
            for group in range(lines.groups):
                block = wide[group * GROUP : (group + 1) * GROUP, :]
                out_ref[:, group * cols + first : group * cols + first + block.shape[1]] = block.astype(jnp.bfloat16)
            if lines.left:
                for lane in range(0, wide.shape[1], HEAD_DIM):
                    block = wide[lines.main : slots, lane : lane + HEAD_DIM]
                    small[pl.ds((first + lane) // HEAD_DIM, lines.left, stride=heads), :] = block
        for number in range(lines.tiles):
            block = small[number * GROUP : (number + 1) * GROUP, :]
            out_ref[:, lines.tile(number)] = block.astype(jnp.bfloat16)


def raise_rows(index, ups, partials, slots, heads, sources):
    lines = Lines(slots, heads)
    return pl.pallas_call(
        functools.partial(raise_kernel, slots, heads, sources, len(ups)),
        out_shape=[jax.ShapeDtypeStruct((GROUP, lines.width), jnp.bfloat16)] * sources,
        in_specs=[VMEM] * (1 + len(ups) + len(partials)),
        out_specs=[VMEM] * sources,
        scratch_shapes=[pltpu.VMEM(lines.small, jnp.float32)],
        compiler_params=PARAMS,
        name="raise_rows",
    )(index, *ups, *partials)


def raise_own_kernel(slots, holders, index_ref, *refs):
    up_refs, partials, out_ref = refs[:holders], refs[holders:-1], refs[-1]
    local_count, rank, cols = up_refs[0].shape
    packed = partials[0][...]
    for other in partials[1:]:
        packed += other[...]
    total = packed[:, packed.shape[1] - index_ref.shape[1] :]
    spread = spread_ranks(index_ref[0:1, :], total, holders, local_count)
    wide = lax.dot_general(spread, stack_ups(up_refs), (((0,), (0,)), ((), ())), preferred_element_type=jnp.float32)
    out_ref[...] = wide[:slots, :]


def raise_own(index, ups, partials, slots):
    return pl.pallas_call(
        functools.partial(raise_own_kernel, slots, len(ups)),
        out_shape=jax.ShapeDtypeStruct((slots, ups[0].shape[2]), jnp.float32),
        in_specs=[VMEM] * (1 + len(ups) + len(partials)),
        out_specs=VMEM,
        compiler_params=PARAMS,
        name="raise_own",
    )(index, *ups, *partials)


def shift(block, axis, offset):
    size = lax.axis_size(axis)
    return lax.ppermute(block, axis, [(i, (i + offset) % size) for i in range(size)])


def swap(block, axis, bits=1):
    size = lax.axis_size(axis)
    return lax.ppermute(block, axis, [(i, i ^ bits) for i in range(size)])


def exchange(block, axis):
    size = lax.axis_size(axis)
    if size & (size - 1):
        return [shift(block, axis, k) for k in range(1, size)]
    return [swap(block, axis, k) for k in [*range(2, size), 1]]


def on_device(queries, past_cache, lengths, live_counts, adapter_index, adapter_down, adapter_up):
    slots, cols = queries.shape
    heads = cols // HEAD_DIM
    replicas = lax.axis_size("replica")
    holders = 2 if replicas % 2 == 0 else 1
    sources = replicas // holders
    pad = 16
    while pad < slots:
        pad *= 2
    downs = [adapter_down] + [swap(adapter_down, "replica") for _ in range(1, holders)]
    rows = attend(queries, past_cache, lengths, adapter_index)
    gathered = [shift(rows, "replica", holders * k) for k in range(1, sources)]
    attention, alive = attention_out(live_counts, rows, slots, heads)
    own = own_lines(rows, slots, heads, pad)
    later_up = lax.optimization_barrier((adapter_up, alive))[0]
    ups = [adapter_up] + [swap(later_up, "replica") for _ in range(1, holders)]
    partial, index = lower(own, downs, gathered, slots, heads, pad)
    partials = [partial] + exchange(partial, "tensor")
    widened = raise_rows(index, ups, partials, slots, heads, sources - 1)
    returned = [shift(widened[k - 1], "replica", -holders * k) for k in range(1, sources)]
    own = raise_own(index, ups, partials, slots)
    adapted = adapted_out(alive, own, returned, slots, heads)
    return (attention, adapted)


def solution(mesh):
    in_specs = (
        P(("groups", "replica"), "tensor"),
        P(None, ("groups", "replica"), None, "tensor"),
        P(("groups", "replica")),
        P(("groups", "replica")),
        P(("groups", "replica")),
        P("replica", None, "tensor"),
        P("replica", None, "tensor"),
    )
    out_specs = (P(("groups", "replica"), "tensor"), P(("groups", "replica"), "tensor"))
    return jax.shard_map(
        on_device, mesh=mesh, in_specs=in_specs, out_specs=out_specs, check_vma=False
    )
```

```python
import functools
import math

import jax
import jax.numpy as jnp
from jax import lax
from jax.experimental import pallas as pl
from jax.experimental.pallas import tpu as pltpu
from jax.sharding import PartitionSpec as P

HEAD_DIM = 128
STAY = 16
SCALING = 2.0
LANES = 128
GROUP = 16
DIGIT = 7

VMEM = pl.BlockSpec(memory_space=pltpu.VMEM)
SMEM = pl.BlockSpec(memory_space=pltpu.SMEM)
HBM = pl.BlockSpec(memory_space=pltpu.HBM)
PARAMS = pltpu.CompilerParams(vmem_limit_bytes=16 * 2**20)


class Lines:
    def __init__(self, slots, heads):
        self.slots, self.heads, self.cols = slots, heads, heads * HEAD_DIM
        self.groups, self.left = divmod(slots, GROUP)
        self.main = self.groups * GROUP
        self.tiles = -(-self.left * heads // GROUP)
        self.start = self.groups * self.cols
        self.width = self.start + self.tiles * HEAD_DIM
        self.small = (max(1, self.tiles) * GROUP, HEAD_DIM)

    def tile(self, number):
        return slice(self.start + number * HEAD_DIM, self.start + (number + 1) * HEAD_DIM)

    def load_left(self, refs, small):
        for number in range(self.tiles):
            total = refs[0][:, self.tile(number)].astype(jnp.float32)
            for ref in refs[1:]:
                total += ref[:, self.tile(number)].astype(jnp.float32)
            small[number * GROUP : (number + 1) * GROUP, :] = total

    def left_rows(self, head, small):
        return small[pl.ds(head, self.left, stride=self.heads), :]

    def column(self, refs, head, small):
        pieces = []
        for group in range(self.groups):
            lanes = slice(group * self.cols + head * HEAD_DIM, group * self.cols + (head + 1) * HEAD_DIM)
            total = refs[0][:, lanes].astype(jnp.float32)
            for ref in refs[1:]:
                total += ref[:, lanes].astype(jnp.float32)
            pieces.append(total)
        if self.left:
            pieces.append(self.left_rows(head, small))
        return jnp.concatenate(pieces, axis=0)


def attend_kernel(
    q_ref, cache_ref, lengths_ref, index_ref, rows_ref,
    q_flat, lengths, index, keys, values, q_rows, o_rows, small, large,
):
    slots, cols = q_ref.shape
    heads = cols // HEAD_DIM
    context, width = keys.shape[1:]
    key_heads = width // HEAD_DIM
    group = heads // key_heads
    fetches = []
    for number, (source, target) in enumerate(((q_ref, q_flat), (lengths_ref, lengths), (index_ref, index))):
        fetches.append(pltpu.make_async_copy(source, target, small.at[number]))
        fetches[-1].start()
    copies = []
    for side, buffer in enumerate((keys, values)):
        copies.append(pltpu.make_async_copy(cache_ref.at[side], buffer, large.at[side]))
        copies[-1].start()
    for fetch in fetches:
        fetch.wait()
    for head in range(heads):
        block = q_flat[:, head * HEAD_DIM : (head + 1) * HEAD_DIM]
        q_rows[pl.ds(head, slots, stride=heads), :] = block.astype(jnp.float32)
    owner = lax.broadcasted_iota(jnp.int32, (heads, HEAD_DIM), 0) // group
    position = lax.broadcasted_iota(jnp.int32, (heads, context), 1)
    weights = []
    copies[0].wait()
    for slot in range(slots):
        rows = q_rows[slot * heads : (slot + 1) * heads, :]
        wide = [jnp.where(owner == k, rows, 0.0) for k in range(key_heads)]
        wide = jnp.concatenate(wide, axis=1).astype(jnp.bfloat16)
        scores = lax.dot_general(
            wide, keys[slot], (((1,), (1,)), ((), ())), preferred_element_type=jnp.float32
        ) / math.sqrt(HEAD_DIM)
        scores = jnp.where(position < lengths[slot], scores, -jnp.inf)
        raised = jnp.exp(scores - jnp.max(scores, axis=-1, keepdims=True))
        weights.append((raised / jnp.sum(raised, axis=-1, keepdims=True)).astype(jnp.bfloat16))
    copies[1].wait()
    for slot in range(slots):
        mixed = jnp.dot(weights[slot], values[slot], preferred_element_type=jnp.float32)
        rows = mixed[:, :HEAD_DIM]
        for k in range(1, key_heads):
            rows = jnp.where(owner == k, mixed[:, k * HEAD_DIM : (k + 1) * HEAD_DIM], rows)
        o_rows[slot * heads : (slot + 1) * heads, :] = rows
    lines = Lines(slots, heads)
    for group in range(lines.groups):
        for head in range(heads):
            lanes = slice(group * cols + head * HEAD_DIM, group * cols + (head + 1) * HEAD_DIM)
            block = o_rows[pl.ds(group * GROUP * heads + head, GROUP, stride=heads), :]
            rows_ref[:, lanes] = block.astype(jnp.bfloat16)
    if lines.tiles * GROUP > lines.left * heads:
        o_rows[slots * heads :, :] = jnp.zeros((lines.tiles * GROUP - lines.left * heads, HEAD_DIM), jnp.float32)
    for number in range(lines.tiles):
        first = lines.main * heads + number * GROUP
        rows_ref[:, lines.tile(number)] = o_rows[first : first + GROUP, :].astype(jnp.bfloat16)
    lane = lax.broadcasted_iota(jnp.int32, (16, LANES), 1)
    line = lax.broadcasted_iota(jnp.int32, (16, LANES), 0)
    named = jnp.zeros((16, LANES), jnp.int32)
    for slot in range(slots):
        named = jnp.where(lane == slot, index[slot], named)
    digits = jnp.where(line == 0, named >> DIGIT, named & ((1 << DIGIT) - 1))
    rows_ref[:, lines.width :] = digits.astype(jnp.float32).astype(jnp.bfloat16)


def attend(queries, past_cache, lengths, adapter_index):
    slots, cols = queries.shape
    heads = cols // HEAD_DIM
    lines = Lines(slots, heads)
    buffer = pltpu.VMEM(past_cache.shape[1:], past_cache.dtype)
    return pl.pallas_call(
        attend_kernel,
        out_shape=jax.ShapeDtypeStruct((GROUP, lines.width + LANES), jnp.bfloat16),
        in_specs=[HBM] * 4,
        out_specs=VMEM,
        scratch_shapes=[
            pltpu.VMEM(queries.shape, queries.dtype),
            pltpu.SMEM(lengths.shape, jnp.int32),
            pltpu.SMEM(adapter_index.shape, jnp.int32),
            buffer,
            buffer,
            pltpu.VMEM((slots * heads, HEAD_DIM), jnp.float32),
            pltpu.VMEM((lines.main * heads + lines.tiles * GROUP, HEAD_DIM), jnp.float32),
            pltpu.SemaphoreType.DMA((3,)),
            pltpu.SemaphoreType.DMA((2,)),
        ],
        cost_estimate=pl.CostEstimate(
            flops=4 * past_cache.size * heads, bytes_accessed=2 * past_cache.size, transcendentals=0
        ),
        compiler_params=PARAMS,
        name="attend",
    )(*[pltpu.with_memory_space_constraint(x, pltpu.HBM) for x in (queries, past_cache, lengths, adapter_index)])


def alive_lines(live_ref, slots):
    slot = lax.broadcasted_iota(jnp.int32, (slots, HEAD_DIM), 0)
    return (slot >= STAY) | (slot < live_ref[0])


def attention_kernel(slots, heads, live_ref, rows_ref, out_ref, alive_ref, small):
    lines = Lines(slots, heads)
    alive = alive_lines(live_ref, slots)
    alive_ref[...] = alive.astype(jnp.float32)
    lines.load_left([rows_ref], small)
    for head in range(heads):
        block = jnp.where(alive, lines.column([rows_ref], head, small), 0.0)
        out_ref[:, head * HEAD_DIM : (head + 1) * HEAD_DIM] = block.astype(out_ref.dtype)


def attention_out(live, rows, slots, heads):
    return pl.pallas_call(
        functools.partial(attention_kernel, slots, heads),
        out_shape=(
            jax.ShapeDtypeStruct((slots, heads * HEAD_DIM), jnp.bfloat16),
            jax.ShapeDtypeStruct((slots, HEAD_DIM), jnp.float32),
        ),
        in_specs=[SMEM, VMEM],
        out_specs=(VMEM, VMEM),
        scratch_shapes=[pltpu.VMEM(Lines(slots, heads).small, jnp.float32)],
        compiler_params=PARAMS,
        name="attention_out",
    )(live, rows)


def adapted_kernel(slots, heads, alive_ref, own_ref, *refs):
    rows_refs, out_ref, small = refs[:-2], refs[-2], refs[-1]
    lines = Lines(slots, heads)
    alive = alive_ref[...] > 0
    if rows_refs:
        lines.load_left(rows_refs, small)
    for head in range(heads):
        block = own_ref[:, head * HEAD_DIM : (head + 1) * HEAD_DIM]
        if rows_refs:
            block += lines.column(rows_refs, head, small)
        out_ref[:, head * HEAD_DIM : (head + 1) * HEAD_DIM] = jnp.where(alive, block, 0.0).astype(out_ref.dtype)


def adapted_out(alive, own, rows, slots, heads):
    return pl.pallas_call(
        functools.partial(adapted_kernel, slots, heads),
        out_shape=jax.ShapeDtypeStruct((slots, heads * HEAD_DIM), jnp.bfloat16),
        in_specs=[VMEM] * (2 + len(rows)),
        out_specs=VMEM,
        scratch_shapes=[pltpu.VMEM(Lines(slots, heads).small, jnp.float32)],
        compiler_params=PARAMS,
        name="adapted_out",
    )(alive, own, *rows)


def first_adapter(holder, local_count):
    return (lax.axis_index("replica") ^ holder) * local_count


def unfold_rows(rows_ref, slots, heads, pad, small, wide_ref, first):
    lines = Lines(slots, heads)
    for group in range(lines.groups):
        at = first + group * GROUP
        wide_ref[at : at + GROUP, :] = rows_ref[:, group * lines.cols : (group + 1) * lines.cols]
    lines.load_left([rows_ref], small)
    if pad > lines.main:
        for head in range(heads):
            block = jnp.zeros((pad - slots, HEAD_DIM), jnp.float32)
            if lines.left:
                block = jnp.concatenate([lines.left_rows(head, small), block], axis=0)
            lanes = slice(head * HEAD_DIM, (head + 1) * HEAD_DIM)
            wide_ref[first + lines.main : first + pad, lanes] = block.astype(jnp.bfloat16)
    digits = rows_ref[:, lines.width :].astype(jnp.float32).astype(jnp.int32)
    return ((digits[0:1, :] << DIGIT) + digits[1:2, :])[:, :pad]


def own_lines_kernel(slots, heads, pad, rows_ref, index_ref, wide_ref, small):
    index_ref[...] = unfold_rows(rows_ref, slots, heads, pad, small, wide_ref, 0)


def own_lines(rows, slots, heads, pad):
    return pl.pallas_call(
        functools.partial(own_lines_kernel, slots, heads, pad),
        out_shape=(
            jax.ShapeDtypeStruct((1, pad), jnp.int32),
            jax.ShapeDtypeStruct((pad, heads * HEAD_DIM), jnp.bfloat16),
        ),
        in_specs=[VMEM],
        out_specs=[VMEM] * 2,
        scratch_shapes=[pltpu.VMEM(Lines(slots, heads).small, jnp.float32)],
        compiler_params=PARAMS,
        name="own_lines",
    )(rows)


def lower_kernel(slots, heads, pad, sources, holders, own_index_ref, own_wide_ref, *refs):
    down_refs, rows_refs = refs[:holders], refs[holders : holders + sources]
    partial_ref, index_ref, small, wide = refs[-4:]
    local_count, rank, cols = down_refs[0].shape
    named = []
    for source in range(sources):
        named.append(unfold_rows(rows_refs[source], slots, heads, pad, small, wide, source * pad))
    named.append(own_index_ref[...])
    for block in range(sources + 1):
        index_ref[block : block + 1, :] = named[block - 1]
    down = jnp.concatenate([ref[...].reshape(local_count * rank, cols) for ref in down_refs], axis=0)
    rows = own_wide_ref[...]
    if sources:
        rows = jnp.concatenate([wide[...], rows], axis=0)
    every = lax.dot_general(down, rows, (((1,), (1,)), ((), ())), preferred_element_type=jnp.float32)
    named = jnp.concatenate(named, axis=1)
    total = jnp.zeros((rank, named.shape[1]), jnp.float32)
    for holder in range(holders):
        for local in range(local_count):
            line = (holder * local_count + local) * rank
            mine = named == first_adapter(holder, local_count) + local
            total += jnp.where(mine, every[line : line + rank, :], 0.0)
    partial_ref[...] = total


def lower(own, downs, rows, slots, heads, pad):
    sources = len(rows)
    rank = downs[0].shape[1]
    return pl.pallas_call(
        functools.partial(lower_kernel, slots, heads, pad, sources, len(downs)),
        out_shape=(
            jax.ShapeDtypeStruct((rank, (1 + sources) * pad), jnp.float32),
            jax.ShapeDtypeStruct((1 + sources, pad), jnp.int32),
        ),
        in_specs=[VMEM] * (2 + len(downs) + sources),
        out_specs=[VMEM] * 2,
        scratch_shapes=[
            pltpu.VMEM(Lines(slots, heads).small, jnp.float32),
            pltpu.VMEM((max(1, sources) * pad, heads * HEAD_DIM), jnp.bfloat16),
        ],
        cost_estimate=pl.CostEstimate(flops=2 * 10**10, bytes_accessed=0, transcendentals=0),
        compiler_params=PARAMS,
        name="lower",
    )(*own, *downs, *rows)


def spread_ranks(index, total, holders, local_count):
    total = SCALING * total
    spread = []
    for holder in range(holders):
        for local in range(local_count):
            mine = index == first_adapter(holder, local_count) + local
            spread.append(jnp.where(mine, total, 0.0))
    return jnp.concatenate(spread, axis=0).astype(jnp.bfloat16)


def stack_ups(up_refs):
    return jnp.concatenate([ref[...].reshape(-1, ref.shape[2]) for ref in up_refs], axis=0)


def raise_kernel(slots, heads, sources, holders, index_ref, *refs):
    up_refs, partials, outs, small = refs[:holders], refs[holders : -sources - 1], refs[-sources - 1 : -1], refs[-1]
    local_count, rank, cols = up_refs[0].shape
    lines = Lines(slots, heads)
    up = stack_ups(up_refs)
    packed = partials[0][...]
    for other in partials[1:]:
        packed += other[...]
    pad = index_ref.shape[1]
    for source in range(sources):
        total = packed[:, source * pad : (source + 1) * pad]
        spread = spread_ranks(index_ref[1 + source : 2 + source, :], total, min(holders, 2), local_count)
        wide = lax.dot_general(spread, up, (((0,), (0,)), ((), ())), preferred_element_type=jnp.float32)
        out_ref = outs[source]
        for group in range(lines.groups):
            block = wide[group * GROUP : (group + 1) * GROUP, :]
            out_ref[:, group * cols : (group + 1) * cols] = block.astype(jnp.bfloat16)
        if lines.left:
            small[...] = jnp.zeros(small.shape, jnp.float32)
            for head in range(heads):
                block = wide[lines.main : slots, head * HEAD_DIM : (head + 1) * HEAD_DIM]
                small[pl.ds(head, lines.left, stride=heads), :] = block
        for number in range(lines.tiles):
            block = small[number * GROUP : (number + 1) * GROUP, :]
            out_ref[:, lines.tile(number)] = block.astype(jnp.bfloat16)


def raise_rows(index, ups, partials, slots, heads, sources):
    lines = Lines(slots, heads)
    return pl.pallas_call(
        functools.partial(raise_kernel, slots, heads, sources, len(ups)),
        out_shape=[jax.ShapeDtypeStruct((GROUP, lines.width), jnp.bfloat16)] * sources,
        in_specs=[VMEM] * (1 + len(ups) + len(partials)),
        out_specs=[VMEM] * sources,
        scratch_shapes=[pltpu.VMEM(lines.small, jnp.float32)],
        compiler_params=PARAMS,
        name="raise_rows",
    )(index, *ups, *partials)


def raise_own_kernel(slots, holders, index_ref, *refs):
    up_refs, partials, out_ref = refs[:holders], refs[holders:-1], refs[-1]
    local_count, rank, cols = up_refs[0].shape
    packed = partials[0][...]
    for other in partials[1:]:
        packed += other[...]
    total = packed[:, packed.shape[1] - index_ref.shape[1] :]
    spread = spread_ranks(index_ref[0:1, :], total, min(holders, 2), local_count)
    wide = lax.dot_general(spread, stack_ups(up_refs), (((0,), (0,)), ((), ())), preferred_element_type=jnp.float32)
    out_ref[...] = wide[:slots, :]


def raise_own(index, ups, partials, slots):
    return pl.pallas_call(
        functools.partial(raise_own_kernel, slots, len(ups)),
        out_shape=jax.ShapeDtypeStruct((slots, ups[0].shape[2]), jnp.float32),
        in_specs=[VMEM] * (1 + len(ups) + len(partials)),
        out_specs=VMEM,
        compiler_params=PARAMS,
        name="raise_own",
    )(index, *ups, *partials)


def shift(block, axis, offset):
    size = lax.axis_size(axis)
    return lax.ppermute(block, axis, [(i, (i + offset) % size) for i in range(size)])


def swap(block, axis, bits=1):
    size = lax.axis_size(axis)
    return lax.ppermute(block, axis, [(i, i ^ bits) for i in range(size)])


def exchange(block, axis):
    size = lax.axis_size(axis)
    if size & (size - 1):
        return [shift(block, axis, k) for k in range(1, size)]
    return [shift(block, axis, k) for k in [*range(2, size), 1]]


def on_device(queries, past_cache, lengths, live_counts, adapter_index, adapter_down, adapter_up):
    slots, cols = queries.shape
    heads = cols // HEAD_DIM
    replicas = lax.axis_size("replica")
    holders = 2 if replicas % 2 == 0 else 1
    sources = replicas // holders
    pad = 16
    while pad < slots:
        pad *= 2
    downs = [adapter_down] + [swap(adapter_down, "replica") for _ in range(1, holders)]
    rows = attend(queries, past_cache, lengths, adapter_index)
    gathered = [shift(rows, "replica", holders * k) for k in range(1, sources)]
    attention, alive = attention_out(live_counts, rows, slots, heads)
    own = own_lines(rows, slots, heads, pad)
    later_up = lax.optimization_barrier((adapter_up, alive))[0]
    half = -(-adapter_up.shape[0] // 2)
    halves = [later_up[:half], later_up[half:]] if holders > 1 else []
    ups = [adapter_up] + [swap(part, "replica") for part in halves if part.shape[0]]
    partial, index = lower(own, downs, gathered, slots, heads, pad)
    partials = [partial] + exchange(partial, "tensor")
    widened = raise_rows(index, ups, partials, slots, heads, sources - 1)
    returned = [shift(widened[k - 1], "replica", -holders * k) for k in range(1, sources)]
    own = raise_own(index, ups, partials, slots)
    adapted = adapted_out(alive, own, returned, slots, heads)
    return (attention, adapted)


def solution(mesh):
    in_specs = (
        P(("groups", "replica"), "tensor"),
        P(None, ("groups", "replica"), None, "tensor"),
        P(("groups", "replica")),
        P(("groups", "replica")),
        P(("groups", "replica")),
        P("replica", None, "tensor"),
        P("replica", None, "tensor"),
    )
    out_specs = (P(("groups", "replica"), "tensor"), P(("groups", "replica"), "tensor"))
    return jax.shard_map(
        on_device, mesh=mesh, in_specs=in_specs, out_specs=out_specs, check_vma=False
    )
```

```python
import functools
import math

import jax
import jax.numpy as jnp
from jax import lax
from jax.experimental import pallas as pl
from jax.experimental.pallas import tpu as pltpu
from jax.sharding import PartitionSpec as P

HEAD_DIM = 128
STAY = 16
SCALING = 2.0
LANES = 128
GROUP = 16
DIGIT = 7

VMEM = pl.BlockSpec(memory_space=pltpu.VMEM)
SMEM = pl.BlockSpec(memory_space=pltpu.SMEM)
HBM = pl.BlockSpec(memory_space=pltpu.HBM)
PARAMS = pltpu.CompilerParams(vmem_limit_bytes=16 * 2**20)


class Lines:
    def __init__(self, slots, heads):
        self.slots, self.heads, self.cols = slots, heads, heads * HEAD_DIM
        self.groups, self.left = divmod(slots, GROUP)
        self.main = self.groups * GROUP
        self.tiles = -(-self.left * heads // GROUP)
        self.start = self.groups * self.cols
        self.width = self.start + self.tiles * HEAD_DIM
        self.small = (max(1, self.tiles) * GROUP, HEAD_DIM)

    def tile(self, number):
        return slice(self.start + number * HEAD_DIM, self.start + (number + 1) * HEAD_DIM)

    def load_left(self, refs, small):
        for number in range(self.tiles):
            total = refs[0][:, self.tile(number)].astype(jnp.float32)
            for ref in refs[1:]:
                total += ref[:, self.tile(number)].astype(jnp.float32)
            small[number * GROUP : (number + 1) * GROUP, :] = total

    def left_rows(self, head, small):
        return small[pl.ds(head, self.left, stride=self.heads), :]

    def column(self, refs, head, small):
        pieces = []
        for group in range(self.groups):
            lanes = slice(group * self.cols + head * HEAD_DIM, group * self.cols + (head + 1) * HEAD_DIM)
            total = refs[0][:, lanes].astype(jnp.float32)
            for ref in refs[1:]:
                total += ref[:, lanes].astype(jnp.float32)
            pieces.append(total)
        if self.left:
            pieces.append(self.left_rows(head, small))
        return jnp.concatenate(pieces, axis=0)


def attend_kernel(
    q_ref, cache_ref, lengths_ref, index_ref, rows_ref,
    q_flat, lengths, index, keys, values, q_rows, o_rows, small, large,
):
    slots, cols = q_ref.shape
    heads = cols // HEAD_DIM
    context, width = keys.shape[1:]
    key_heads = width // HEAD_DIM
    group = heads // key_heads
    fetches = []
    for number, (source, target) in enumerate(((q_ref, q_flat), (lengths_ref, lengths), (index_ref, index))):
        fetches.append(pltpu.make_async_copy(source, target, small.at[number]))
        fetches[-1].start()
    copies = []
    for side, buffer in enumerate((keys, values)):
        copies.append(pltpu.make_async_copy(cache_ref.at[side], buffer, large.at[side]))
        copies[-1].start()
    for fetch in fetches:
        fetch.wait()
    for head in range(heads):
        block = q_flat[:, head * HEAD_DIM : (head + 1) * HEAD_DIM]
        q_rows[pl.ds(head, slots, stride=heads), :] = block.astype(jnp.float32)
    owner = lax.broadcasted_iota(jnp.int32, (heads, HEAD_DIM), 0) // group
    position = lax.broadcasted_iota(jnp.int32, (heads, context), 1)
    weights = []
    copies[0].wait()
    for slot in range(slots):
        rows = q_rows[slot * heads : (slot + 1) * heads, :]
        wide = [jnp.where(owner == k, rows, 0.0) for k in range(key_heads)]
        wide = jnp.concatenate(wide, axis=1).astype(jnp.bfloat16)
        scores = lax.dot_general(
            wide, keys[slot], (((1,), (1,)), ((), ())), preferred_element_type=jnp.float32
        ) / math.sqrt(HEAD_DIM)
        scores = jnp.where(position < lengths[slot], scores, -jnp.inf)
        raised = jnp.exp(scores - jnp.max(scores, axis=-1, keepdims=True))
        weights.append((raised / jnp.sum(raised, axis=-1, keepdims=True)).astype(jnp.bfloat16))
    copies[1].wait()
    for slot in range(slots):
        mixed = jnp.dot(weights[slot], values[slot], preferred_element_type=jnp.float32)
        rows = mixed[:, :HEAD_DIM]
        for k in range(1, key_heads):
            rows = jnp.where(owner == k, mixed[:, k * HEAD_DIM : (k + 1) * HEAD_DIM], rows)
        o_rows[slot * heads : (slot + 1) * heads, :] = rows
    lines = Lines(slots, heads)
    for group in range(lines.groups):
        for head in range(heads):
            lanes = slice(group * cols + head * HEAD_DIM, group * cols + (head + 1) * HEAD_DIM)
            block = o_rows[pl.ds(group * GROUP * heads + head, GROUP, stride=heads), :]
            rows_ref[:, lanes] = block.astype(jnp.bfloat16)
    if lines.tiles * GROUP > lines.left * heads:
        o_rows[slots * heads :, :] = jnp.zeros((lines.tiles * GROUP - lines.left * heads, HEAD_DIM), jnp.float32)
    for number in range(lines.tiles):
        first = lines.main * heads + number * GROUP
        rows_ref[:, lines.tile(number)] = o_rows[first : first + GROUP, :].astype(jnp.bfloat16)
    lane = lax.broadcasted_iota(jnp.int32, (16, LANES), 1)
    line = lax.broadcasted_iota(jnp.int32, (16, LANES), 0)
    named = jnp.zeros((16, LANES), jnp.int32)
    for slot in range(slots):
        named = jnp.where(lane == slot, index[slot], named)
    digits = jnp.where(line == 0, named >> DIGIT, named & ((1 << DIGIT) - 1))
    rows_ref[:, lines.width :] = digits.astype(jnp.float32).astype(jnp.bfloat16)


def attend(queries, past_cache, lengths, adapter_index):
    slots, cols = queries.shape
    heads = cols // HEAD_DIM
    lines = Lines(slots, heads)
    buffer = pltpu.VMEM(past_cache.shape[1:], past_cache.dtype)
    return pl.pallas_call(
        attend_kernel,
        out_shape=jax.ShapeDtypeStruct((GROUP, lines.width + LANES), jnp.bfloat16),
        in_specs=[HBM] * 4,
        out_specs=VMEM,
        scratch_shapes=[
            pltpu.VMEM(queries.shape, queries.dtype),
            pltpu.SMEM(lengths.shape, jnp.int32),
            pltpu.SMEM(adapter_index.shape, jnp.int32),
            buffer,
            buffer,
            pltpu.VMEM((slots * heads, HEAD_DIM), jnp.float32),
            pltpu.VMEM((lines.main * heads + lines.tiles * GROUP, HEAD_DIM), jnp.float32),
            pltpu.SemaphoreType.DMA((3,)),
            pltpu.SemaphoreType.DMA((2,)),
        ],
        cost_estimate=pl.CostEstimate(
            flops=4 * past_cache.size * heads, bytes_accessed=2 * past_cache.size, transcendentals=0
        ),
        compiler_params=PARAMS,
        name="attend",
    )(*[pltpu.with_memory_space_constraint(x, pltpu.HBM) for x in (queries, past_cache, lengths, adapter_index)])


def alive_lines(live_ref, slots):
    slot = lax.broadcasted_iota(jnp.int32, (slots, HEAD_DIM), 0)
    return (slot >= STAY) | (slot < live_ref[0])


def attention_kernel(slots, heads, live_ref, rows_ref, out_ref, alive_ref, small):
    lines = Lines(slots, heads)
    alive = alive_lines(live_ref, slots)
    alive_ref[...] = alive.astype(jnp.float32)
    lines.load_left([rows_ref], small)
    for head in range(heads):
        block = jnp.where(alive, lines.column([rows_ref], head, small), 0.0)
        out_ref[:, head * HEAD_DIM : (head + 1) * HEAD_DIM] = block.astype(out_ref.dtype)


def attention_out(live, rows, slots, heads):
    return pl.pallas_call(
        functools.partial(attention_kernel, slots, heads),
        out_shape=(
            jax.ShapeDtypeStruct((slots, heads * HEAD_DIM), jnp.bfloat16),
            jax.ShapeDtypeStruct((slots, HEAD_DIM), jnp.float32),
        ),
        in_specs=[SMEM, VMEM],
        out_specs=(VMEM, VMEM),
        scratch_shapes=[pltpu.VMEM(Lines(slots, heads).small, jnp.float32)],
        compiler_params=PARAMS,
        name="attention_out",
    )(live, rows)


def adapted_kernel(slots, heads, alive_ref, own_ref, *refs):
    rows_refs, out_ref, small = refs[:-2], refs[-2], refs[-1]
    lines = Lines(slots, heads)
    alive = alive_ref[...] > 0
    if rows_refs:
        lines.load_left(rows_refs, small)
    for head in range(heads):
        block = own_ref[:, head * HEAD_DIM : (head + 1) * HEAD_DIM]
        if rows_refs:
            block += lines.column(rows_refs, head, small)
        out_ref[:, head * HEAD_DIM : (head + 1) * HEAD_DIM] = jnp.where(alive, block, 0.0).astype(out_ref.dtype)


def adapted_out(alive, own, rows, slots, heads):
    return pl.pallas_call(
        functools.partial(adapted_kernel, slots, heads),
        out_shape=jax.ShapeDtypeStruct((slots, heads * HEAD_DIM), jnp.bfloat16),
        in_specs=[VMEM] * (2 + len(rows)),
        out_specs=VMEM,
        scratch_shapes=[pltpu.VMEM(Lines(slots, heads).small, jnp.float32)],
        compiler_params=PARAMS,
        name="adapted_out",
    )(alive, own, *rows)


def first_adapter(holder, local_count):
    return (lax.axis_index("replica") ^ holder) * local_count


def unfold_rows(rows_ref, slots, heads, pad, small, wide_ref, first):
    lines = Lines(slots, heads)
    for group in range(lines.groups):
        at = first + group * GROUP
        wide_ref[at : at + GROUP, :] = rows_ref[:, group * lines.cols : (group + 1) * lines.cols]
    lines.load_left([rows_ref], small)
    if pad > lines.main:
        for head in range(heads):
            block = jnp.zeros((pad - slots, HEAD_DIM), jnp.float32)
            if lines.left:
                block = jnp.concatenate([lines.left_rows(head, small), block], axis=0)
            lanes = slice(head * HEAD_DIM, (head + 1) * HEAD_DIM)
            wide_ref[first + lines.main : first + pad, lanes] = block.astype(jnp.bfloat16)
    digits = rows_ref[:, lines.width :].astype(jnp.float32).astype(jnp.int32)
    return ((digits[0:1, :] << DIGIT) + digits[1:2, :])[:, :pad]


def own_lines_kernel(slots, heads, pad, rows_ref, index_ref, wide_ref, small):
    index_ref[...] = unfold_rows(rows_ref, slots, heads, pad, small, wide_ref, 0)


def own_lines(rows, slots, heads, pad):
    return pl.pallas_call(
        functools.partial(own_lines_kernel, slots, heads, pad),
        out_shape=(
            jax.ShapeDtypeStruct((1, pad), jnp.int32),
            jax.ShapeDtypeStruct((pad, heads * HEAD_DIM), jnp.bfloat16),
        ),
        in_specs=[VMEM],
        out_specs=[VMEM] * 2,
        scratch_shapes=[pltpu.VMEM(Lines(slots, heads).small, jnp.float32)],
        compiler_params=PARAMS,
        name="own_lines",
    )(rows)


def lower_kernel(slots, heads, pad, sources, holders, own_index_ref, own_wide_ref, *refs):
    down_refs, rows_refs = refs[:holders], refs[holders : holders + sources]
    partial_ref, index_ref, small, wide = refs[-4:]
    local_count, rank, cols = down_refs[0].shape
    named = []
    for source in range(sources):
        named.append(unfold_rows(rows_refs[source], slots, heads, pad, small, wide, source * pad))
    named.append(own_index_ref[...])
    for block in range(sources + 1):
        index_ref[block : block + 1, :] = named[block - 1]
    down = jnp.concatenate([ref[...].reshape(local_count * rank, cols) for ref in down_refs], axis=0)
    lines = Lines(slots, heads)
    blocks = []
    for source in range(sources):
        for group in range(lines.groups):
            blocks.append(rows_refs[source][:, group * cols : (group + 1) * cols])
        if pad > lines.main:
            blocks.append(wide[source * pad + lines.main : (source + 1) * pad, :])
    rows = jnp.concatenate(blocks + [own_wide_ref[...]], axis=0)
    every = lax.dot_general(down, rows, (((1,), (1,)), ((), ())), preferred_element_type=jnp.float32)
    named = jnp.concatenate(named, axis=1)
    total = jnp.zeros((rank, named.shape[1]), jnp.float32)
    for holder in range(holders):
        for local in range(local_count):
            line = (holder * local_count + local) * rank
            mine = named == first_adapter(holder, local_count) + local
            total += jnp.where(mine, every[line : line + rank, :], 0.0)
    partial_ref[...] = total


def lower(own, downs, rows, slots, heads, pad):
    sources = len(rows)
    rank = downs[0].shape[1]
    return pl.pallas_call(
        functools.partial(lower_kernel, slots, heads, pad, sources, len(downs)),
        out_shape=(
            jax.ShapeDtypeStruct((rank, (1 + sources) * pad), jnp.float32),
            jax.ShapeDtypeStruct((1 + sources, pad), jnp.int32),
        ),
        in_specs=[VMEM] * (2 + len(downs) + sources),
        out_specs=[VMEM] * 2,
        scratch_shapes=[
            pltpu.VMEM(Lines(slots, heads).small, jnp.float32),
            pltpu.VMEM((max(1, sources) * pad, heads * HEAD_DIM), jnp.bfloat16),
        ],
        cost_estimate=pl.CostEstimate(flops=2 * 10**10, bytes_accessed=0, transcendentals=0),
        compiler_params=PARAMS,
        name="lower",
    )(*own, *downs, *rows)


def spread_ranks(index, total, holders, local_count):
    total = SCALING * total
    spread = []
    for holder in range(holders):
        for local in range(local_count):
            mine = index == first_adapter(holder, local_count) + local
            spread.append(jnp.where(mine, total, 0.0))
    return jnp.concatenate(spread, axis=0).astype(jnp.bfloat16)


def stack_ups(up_refs):
    return jnp.concatenate([ref[...].reshape(-1, ref.shape[2]) for ref in up_refs], axis=0)


def raise_kernel(slots, heads, sources, holders, index_ref, *refs):
    up_refs, partials, outs, small = refs[:holders], refs[holders : -sources - 1], refs[-sources - 1 : -1], refs[-1]
    local_count, rank, cols = up_refs[0].shape
    lines = Lines(slots, heads)
    up = stack_ups(up_refs)
    packed = partials[0][...]
    for other in partials[1:]:
        packed += other[...]
    pad = index_ref.shape[1]
    for source in range(sources):
        total = packed[:, source * pad : (source + 1) * pad]
        spread = spread_ranks(index_ref[1 + source : 2 + source, :], total, min(holders, 2), local_count)
        wide = lax.dot_general(spread, up, (((0,), (0,)), ((), ())), preferred_element_type=jnp.float32)
        out_ref = outs[source]
        for group in range(lines.groups):
            block = wide[group * GROUP : (group + 1) * GROUP, :]
            out_ref[:, group * cols : (group + 1) * cols] = block.astype(jnp.bfloat16)
        if lines.left:
            small[...] = jnp.zeros(small.shape, jnp.float32)
            for head in range(heads):
                block = wide[lines.main : slots, head * HEAD_DIM : (head + 1) * HEAD_DIM]
                small[pl.ds(head, lines.left, stride=heads), :] = block
        for number in range(lines.tiles):
            block = small[number * GROUP : (number + 1) * GROUP, :]
            out_ref[:, lines.tile(number)] = block.astype(jnp.bfloat16)


def raise_rows(index, ups, partials, slots, heads, sources):
    lines = Lines(slots, heads)
    return pl.pallas_call(
        functools.partial(raise_kernel, slots, heads, sources, len(ups)),
        out_shape=[jax.ShapeDtypeStruct((GROUP, lines.width), jnp.bfloat16)] * sources,
        in_specs=[VMEM] * (1 + len(ups) + len(partials)),
        out_specs=[VMEM] * sources,
        scratch_shapes=[pltpu.VMEM(lines.small, jnp.float32)],
        compiler_params=PARAMS,
        name="raise_rows",
    )(index, *ups, *partials)


def raise_own_kernel(slots, holders, index_ref, *refs):
    up_refs, partials, out_ref = refs[:holders], refs[holders:-1], refs[-1]
    local_count, rank, cols = up_refs[0].shape
    packed = partials[0][...]
    for other in partials[1:]:
        packed += other[...]
    total = packed[:, packed.shape[1] - index_ref.shape[1] :]
    spread = spread_ranks(index_ref[0:1, :], total, min(holders, 2), local_count)
    wide = lax.dot_general(spread, stack_ups(up_refs), (((0,), (0,)), ((), ())), preferred_element_type=jnp.float32)
    out_ref[...] = wide[:slots, :]


def raise_own(index, ups, partials, slots):
    return pl.pallas_call(
        functools.partial(raise_own_kernel, slots, len(ups)),
        out_shape=jax.ShapeDtypeStruct((slots, ups[0].shape[2]), jnp.float32),
        in_specs=[VMEM] * (1 + len(ups) + len(partials)),
        out_specs=VMEM,
        compiler_params=PARAMS,
        name="raise_own",
    )(index, *ups, *partials)


def shift(block, axis, offset):
    size = lax.axis_size(axis)
    return lax.ppermute(block, axis, [(i, (i + offset) % size) for i in range(size)])


def swap(block, axis, bits=1):
    size = lax.axis_size(axis)
    return lax.ppermute(block, axis, [(i, i ^ bits) for i in range(size)])


def exchange(block, axis):
    size = lax.axis_size(axis)
    if size & (size - 1):
        return [shift(block, axis, k) for k in range(1, size)]
    return [shift(block, axis, k) for k in [*range(2, size), 1]]


def on_device(queries, past_cache, lengths, live_counts, adapter_index, adapter_down, adapter_up):
    slots, cols = queries.shape
    heads = cols // HEAD_DIM
    replicas = lax.axis_size("replica")
    holders = 2 if replicas % 2 == 0 else 1
    sources = replicas // holders
    pad = 16
    while pad < slots:
        pad *= 2
    downs = [adapter_down] + [swap(adapter_down, "replica") for _ in range(1, holders)]
    rows = attend(queries, past_cache, lengths, adapter_index)
    gathered = [shift(rows, "replica", holders * k) for k in range(1, sources)]
    attention, alive = attention_out(live_counts, rows, slots, heads)
    own = own_lines(rows, slots, heads, pad)
    later_up = lax.optimization_barrier((adapter_up, alive))[0]
    half = -(-adapter_up.shape[0] // 2)
    halves = [later_up[:half], later_up[half:]] if holders > 1 else []
    ups = [adapter_up] + [swap(part, "replica") for part in halves if part.shape[0]]
    partial, index = lower(own, downs, gathered, slots, heads, pad)
    partials = [partial] + exchange(partial, "tensor")
    widened = raise_rows(index, ups, partials, slots, heads, sources - 1)
    returned = [shift(widened[k - 1], "replica", -holders * k) for k in range(1, sources)]
    own = raise_own(index, ups, partials, slots)
    adapted = adapted_out(alive, own, returned, slots, heads)
    return (attention, adapted)


def solution(mesh):
    in_specs = (
        P(("groups", "replica"), "tensor"),
        P(None, ("groups", "replica"), None, "tensor"),
        P(("groups", "replica")),
        P(("groups", "replica")),
        P(("groups", "replica")),
        P("replica", None, "tensor"),
        P("replica", None, "tensor"),
    )
    out_specs = (P(("groups", "replica"), "tensor"), P(("groups", "replica"), "tensor"))
    return jax.shard_map(
        on_device, mesh=mesh, in_specs=in_specs, out_specs=out_specs, check_vma=False
    )
```
